256 devices in a mesh: rep: 16 (over z, y_hi), seq: 16 (over x, y_lo, core).
Axes of the slice: x: 4, y: 4 (y_hi: 2, y_lo: 2; y = y_hi * 2 + y_lo), z: 8, core: 2. Of those that a mesh axis runs over, the one named last changes fastest.
Arguments:
- tokens: bfloat16 [131072, 4096], P(('rep', 'seq')), may hold values from -24 to 24
- w_query: bfloat16 [4096, 256], P('rep'), may hold values from -0.09375 to 0.09375
- w_key: bfloat16 [4096, 256], P('rep'), may hold values from -0.09375 to 0.09375
- w_value: bfloat16 [4096, 256], P('rep'), may hold values from -0.09375 to 0.09375
- cotangent: bfloat16 [131072, 256], P(('rep', 'seq')), may hold values from -6 to 6
Outputs:
- attended: bfloat16 [131072, 256], P(('rep', 'seq'))
- grad_tokens: bfloat16 [131072, 4096], P(('rep', 'seq'))
- grad_query: float32 [4096, 256], P(('rep', 'seq'))
- grad_key: float32 [4096, 256], P(('rep', 'seq'))
- grad_value: float32 [4096, 256], P(('rep', 'seq'))
The draws below stay inside these ranges and needn't reach their ends.
All inputs are finite; a program needn't handle non-finite values.
Results may differ from the reference program's by a relative error of at most 0.015.
Values may be sent and summed in bfloat16 or wider, within the bound.
A program may use at most 128 MiB of HBM per device.

```python
import jax
import jax.numpy as jnp
from jax import lax

D = 4096
HEADS = 2
HD = 128
BLOCK = 512
T_DEV = 512
HW = 256
LEN = 8192
TOKENS = 131072
N_REP = 16


def spiked(values, own_key, source, target, shards_of, factor):
    owner, partner = [(jnp.arange(values.shape[position]) // (values.shape[position] // shards_of)).reshape([-1 if axis == position else 1 for axis in range(values.ndim)]) for position in (source, target)]
    chosen = jax.random.permutation(own_key, shards_of)[partner]
    strong = (owner == chosen) | (owner == (partner + shards_of // 2) % shards_of)
    return jnp.where(strong, factor * values, values)


def block_levels(own_key, dims, split, least, largest):
    level, own = 1.0, jax.random.fold_in(own_key, 6)
    for position, blocks in split:
        heights = jnp.exp(jax.random.uniform(jax.random.fold_in(own, position), (blocks,), jnp.float32, least / len(split), largest / len(split)))
        level = level * jnp.repeat(heights, dims[position] // blocks).reshape([-1 if axis == position else 1 for axis in range(len(dims))])
    return level


def scatter_about(rng, dims, spread, most, cuts=(), kind=jnp.bfloat16):
    gain = block_levels(rng, dims, cuts, -0.22, 0.18) if cuts else 1.0
    entries = jax.random.normal(rng, dims, jnp.float32) * spread * gain
    return jnp.minimum(jnp.maximum(entries, -most), most).astype(kind)


def gaussian_with(key, dims, spread, reach, cuts, heavy, kind=jnp.bfloat16):
    entries = spread * jax.random.normal(key, dims, jnp.float32)
    if cuts:
        entries = entries * block_levels(key, dims, cuts, -0.22, 0.18)
    return jnp.clip(spiked(entries, jax.random.fold_in(key, 3), *heavy), -reach, reach).astype(kind)


def setup_inputs(seed: int = 0) -> dict:
    key_list = jax.random.split(jax.random.key(seed), 6)
    return {
        "tokens": gaussian_with(key_list[0], (TOKENS, D), 1.0, 24.0, ((0, 256),), (0, 1, 256, 6.0)),
        "w_query": scatter_about(key_list[1], (D, HW), D ** -0.5, 0.09375, ((0, 16),)),
        "w_key": scatter_about(key_list[2], (D, HW), D ** -0.5, 0.09375, ((0, 16),)),
        "w_value": scatter_about(key_list[3], (D, HW), D ** -0.5, 0.09375, ((0, 16),)),
        "cotangent": scatter_about(key_list[4], (TOKENS, HW), 1.0, 6.0, ((0, 256),)),
    }


EPS = 1e-06
highest = lax.Precision.HIGHEST

def exclusive_sum(terms):
    running = jnp.cumsum(terms, 0)
    return jnp.concatenate([jnp.zeros_like(terms[:1]), running[:-1]], 0)

def rounded(values):
    return lax.optimization_barrier(values.astype(jnp.bfloat16)).astype(jnp.float32)

def one_sequence(seq_tokens, w_query, w_key, w_value, seq_grad):
    length_rows = seq_tokens.shape[0]
    blocks = length_rows // BLOCK
    shape4 = (blocks, BLOCK, HEADS, HD)
    q_blocks = rounded(jnp.dot(seq_tokens, w_query, preferred_element_type=jnp.float32)).reshape(shape4)
    k_blocks = rounded(jnp.dot(seq_tokens, w_key, preferred_element_type=jnp.float32)).reshape(shape4)
    v_blocks = rounded(jnp.dot(seq_tokens, w_value, preferred_element_type=jnp.float32)).reshape(shape4)
    block_states = jnp.einsum('bshd,bshe->bhde', k_blocks, v_blocks, precision=highest)
    prior_state = exclusive_sum(block_states)
    causal = lax.broadcasted_iota(jnp.int32, (BLOCK, BLOCK), 0) >= lax.broadcasted_iota(jnp.int32, (BLOCK, BLOCK), 1)
    scores = rounded(jnp.where(causal, jnp.einsum('bthd,bshd->bhts', q_blocks, k_blocks, precision=highest), 0.0))
    att_mix = jnp.einsum('bhts,bshd->bthd', scores, v_blocks, precision=highest) + jnp.einsum('bthd,bhde->bthe', q_blocks, prior_state, precision=highest)
    norm_scale = lax.rsqrt(lax.optimization_barrier(jnp.mean(att_mix * att_mix, -1, keepdims=True)) + EPS)
    attended = (att_mix * norm_scale).astype(jnp.bfloat16).reshape(length_rows, HEADS * HD)
    grad_out = seq_grad.astype(jnp.float32).reshape(shape4)
    grad_dot = lax.optimization_barrier(jnp.mean(grad_out * att_mix, -1, keepdims=True))
    grad_mixed = rounded(norm_scale * grad_out - norm_scale * norm_scale * norm_scale * att_mix * grad_dot)
    block_back = jnp.einsum('bthd,bthe->bhde', q_blocks, grad_mixed, precision=highest)
    later_state = exclusive_sum(block_back[::-1])[::-1]
    back_scores = rounded(jnp.where(causal, jnp.einsum('bthe,bshe->bhts', grad_mixed, v_blocks, precision=highest), 0.0))
    grad_q = jnp.einsum('bhts,bshd->bthd', back_scores, k_blocks, precision=highest) + jnp.einsum('bthe,bhde->bthd', grad_mixed, prior_state, precision=highest)
    grad_k = jnp.einsum('bhts,bthd->bshd', back_scores, q_blocks, precision=highest) + jnp.einsum('bshe,bhde->bshd', v_blocks, later_state, precision=highest)
    grad_v = jnp.einsum('bhts,bthe->bshe', scores, grad_mixed, precision=highest) + jnp.einsum('bshd,bhde->bshe', k_blocks, later_state, precision=highest)
    grad_q = grad_q.astype(jnp.bfloat16).reshape(length_rows, HEADS * HD)
    grad_k = grad_k.astype(jnp.bfloat16).reshape(length_rows, HEADS * HD)
    grad_v = grad_v.astype(jnp.bfloat16).reshape(length_rows, HEADS * HD)
    d_tokens = jnp.dot(grad_q, w_query.T, preferred_element_type=jnp.float32)
    d_tokens = d_tokens + jnp.dot(grad_k, w_key.T, preferred_element_type=jnp.float32)
    d_tokens = d_tokens + jnp.dot(grad_v, w_value.T, preferred_element_type=jnp.float32)
    stacked = jnp.concatenate([grad_q, grad_k, grad_v], 1)
    weight_terms = jnp.dot(seq_tokens.T, stacked, preferred_element_type=jnp.float32)
    return (attended, d_tokens.astype(jnp.bfloat16), weight_terms)

def reference(tokens, w_query, w_key, w_value, cotangent):
    token_seqs = tokens.reshape(N_REP, LEN, D)
    grad_seqs = cotangent.reshape(N_REP, LEN, HEADS * HD)

    def one_step(carry, pieces):
        attended, d_tokens, weight_terms = one_sequence(pieces[0], w_query, w_key, w_value, pieces[1])
        return (carry + weight_terms, (attended, d_tokens))
    start_sum = jnp.zeros((D, 3 * HEADS * HD), jnp.float32)
    summed, outputs = lax.scan(one_step, start_sum, (token_seqs, grad_seqs))
    summed = summed * (1.0 / T_DEV)
    att_width = HEADS * HD
    attended = outputs[0].reshape(TOKENS, att_width)
    grad_tokens = outputs[1].reshape(TOKENS, D)
    return (attended, grad_tokens, summed[:, :att_width], summed[:, att_width:2 * att_width], summed[:, 2 * att_width:])
```

```python
import jax
import jax.numpy as jnp
from jax import lax
from jax.experimental import pallas as pl
from jax.experimental.pallas import tpu as pltpu
from jax.sharding import PartitionSpec as P

D = 4096
HD = 128
T_DEV = 512
EPS = 1e-06
MESH = pl.DeviceIdType.MESH
f32 = jnp.float32
bf16 = jnp.bfloat16
N_SEM = 160
BLK = (8, 2, 4, 2, 32, 128)


def mod(a, n):
    return lax.rem(a, jnp.int32(n))


def dot(a, b, ca=1, cb=0):
    return lax.dot_general(a, b, (((ca,), (cb,)), ((), ())), preferred_element_type=f32)


def split(a):
    hi = a.astype(bf16)
    return hi, (a - hi.astype(f32)).astype(bf16)


class Net:
    def __init__(self, send_sems, recv_sems):
        self.ss, self.rs, self.n, self.open = send_sems, recv_sems, 0, []

    def make(self, src, dst, to):
        i = self.n
        self.n += 1
        assert i < N_SEM
        return pltpu.make_async_remote_copy(
            src_ref=src, dst_ref=dst, send_sem=self.ss.at[i], recv_sem=self.rs.at[i], device_id=to, device_id_type=MESH
        )

    def send(self, src, dst, to):
        cp = self.make(src, dst, to)
        cp.start()
        self.open.append((cp, None))
        return cp

    def send_if(self, cond, src, dst, to):
        cp = self.make(src, dst, to)
        pl.when(cond)(cp.start)
        self.open.append((cp, cond))
        return cp

    def finish(self):
        for cp, cond in self.open:
            if cond is None:
                cp.wait_send()
            else:
                pl.when(cond)(cp.wait_send)


def kernel(
    tok_hbm, wq, wk, wv, cot, att_o, gt_hbm, gq_o, gk_o, gv_o,
    tok, w0, w1, w2, o0, o1, o2, qkv, cotb, scores, mixl, dmix, d_all, d_oth, att_oth, att_snd,
    st_snd, st_rcv, bk_snd, bk_rcv, prior, later,
    p0, p1, p2, sa, ra, sb, rb, sc, rc, acc_a, acc_b, acc_c,
    sa_y, ra_y, sa_x, ra_x, acc_a2, sb_y, rb_y, sb_z, rb_z, acc_b2, sc_x, rc_x, sc_z, rc_z, acc_c2,
    fin, fin_oth, gt_buf, send_sems, recv_sems, loc_sems,
):
    rep, seq = lax.axis_index("rep"), lax.axis_index("seq")
    z, yh = lax.div(rep, jnp.int32(2)), mod(rep, 2)
    x, yl, c = lax.div(seq, jnp.int32(4)), mod(lax.div(seq, jnp.int32(2)), 2), mod(seq, 2)
    y = yh * 2 + yl
    oc = 1 - c

    def dev(x_, y_, z_, c_):
        return {"rep": z_ * 2 + lax.div(y_, jnp.int32(2)), "seq": x_ * 4 + mod(y_, 2) * 2 + c_}

    def xd(k):
        return dev(mod(x + k, 4), y, z, c)

    def yd(k):
        return dev(x, mod(y + k, 4), z, c)

    def zd(k):
        return dev(x, y, mod(z + k, 8), c)

    partner = dev(x, y, z, oc)
    across = dev(x, 3 - y, z, c)
    group = [(dx, dl) for dx in range(4) for dl in range(2) if dx or dl]

    def gd(dx, dl):
        return dev(mod(x + dx, 4), yh * 2 + mod(yl + dl, 2), z, c)

    def place(dx, dl):
        return mod(x + dx, 4) * 2 + mod(yl + dl, 2)

    here = x * 2 + yl

    tok_cp = pltpu.make_async_copy(tok_hbm, tok.at[pl.ds(pl.multiple_of(c * 512, 512), 512)], loc_sems.at[0])
    tok_cp.start()
    peers = [partner] + [xd(k) for k in (1, 2, 3)] + [yd(k) for k in (1, 2, 3)] + [zd(k) for k in range(1, 8)]
    peers += [gd(dx, 1) for dx in (1, 2, 3)]
    bar = pltpu.get_barrier_semaphore()
    lane_c = pl.ds(pl.multiple_of(c * HD, HD), HD)
    lane_o = pl.ds(pl.multiple_of(oc * HD, HD), HD)
    for w, src in ((w0, wq), (w1, wk), (w2, wv)):
        w[z, yh] = src[:, lane_c].reshape(BLK[2:])
    for to in peers:
        pl.semaphore_signal(bar, inc=1, device_id=to, device_id_type=MESH)
    cotb[c] = cot[:, lane_c]
    pl.semaphore_wait(bar, len(peers))

    net = Net(send_sems, recv_sems)

    b_z = [net.send(w1.at[z, yh, x, yl], w1.at[z, yh, x, yl], zd(k)) for k in (1, 7, 2, 6, 3, 5, 4)]
    c_z = [net.send(w2.at[z, yh, x, yl], w2.at[z, yh, x, yl], zd(k)) for k in (1, 7, 2, 6, 3, 5, 4)]
    a_y = net.send(w0.at[z, yh], w0.at[z, yh], across)
    oyh = 1 - yh

    def a_send(at, half, k):
        return net.send(w0.at[at, half], w0.at[at, half], zd(k))

    a1 = [a_send(z, yh, 1), a_send(z, yh, 7)]
    cot_cp = net.send(cot.at[:, lane_o], cotb.at[c], partner)
    tok_x = net.send(tok_hbm, tok.at[pl.ds(pl.multiple_of(c * 512, 512), 512)], partner)
    a_y.wait_recv()
    a1 += [a_send(z, oyh, 1), a_send(z, oyh, 7)]
    for cp in b_z:
        cp.wait_recv()
    all_z = pl.ds(0, 8)
    b_y = [net.send(w1.at[all_z, yh, x, yl], w1.at[all_z, yh, x, yl], yd(k)) for k in (1, 3, 2)]
    for cp in c_z:
        cp.wait_recv()
    c_x = [net.send(w2.at[all_z, yh, x, yl], w2.at[all_z, yh, x, yl], xd(k)) for k in (1, 3, 2)]

    def a_step(prev, k):
        out = []
        for i, half in ((0, yh), (2, oyh)):
            prev[i].wait_recv()
            out.append(a_send(mod(z + 8 - k, 8), half, 1))
            prev[i + 1].wait_recv()
            out.append(a_send(mod(z + k, 8), half, 7))
        return out

    a2 = a_step(a1, 1)
    lo, hi = pl.ds(0, 4), pl.ds(4, 4)
    for cp in b_y:
        cp.wait_recv()
    b_x = []
    for first, second in ((lo, hi),):
        b_x.append(net.send(w1.at[first, :, x], w1.at[first, :, x], xd(1)))
        b_x.append(net.send(w1.at[second, :, x], w1.at[second, :, x], xd(3)))
        b_x.append(net.send(w1.at[second, :, x], w1.at[second, :, x], xd(1)))
        b_x.append(net.send(w1.at[first, :, x], w1.at[first, :, x], xd(3)))
    for cp in c_x:
        cp.wait_recv()
    c_y = [
        net.send(w2.at[lo, yh, :, yl], w2.at[lo, yh, :, yl], yd(1)),
        net.send(w2.at[hi, yh, :, yl], w2.at[hi, yh, :, yl], yd(3)),
        net.send(w2.at[hi, yh, :, yl], w2.at[hi, yh, :, yl], yd(1)),
        net.send(w2.at[lo, yh, :, yl], w2.at[lo, yh, :, yl], yd(3)),
    ]
    a3 = a_step(a2, 2)
    b_x[0].wait_recv()
    xm, xp = mod(x + 3, 4), mod(x + 1, 4)
    b_f = [net.send(w1.at[lo, :, xm], w1.at[lo, :, xm], xd(1))]
    b_x[1].wait_recv()
    b_f += [net.send(w1.at[hi, :, xp], w1.at[hi, :, xp], xd(3))]
    ym, yp = mod(y + 3, 4), mod(y + 1, 4)
    ymh, yml, yph, ypl = lax.div(ym, jnp.int32(2)), mod(ym, 2), lax.div(yp, jnp.int32(2)), mod(yp, 2)
    c_y[0].wait_recv()
    c_f = [net.send(w2.at[lo, ymh, :, yml], w2.at[lo, ymh, :, yml], yd(1))]
    c_y[1].wait_recv()
    c_f += [net.send(w2.at[hi, yph, :, ypl], w2.at[hi, yph, :, ypl], yd(3))]
    for cp in a3:
        cp.wait_recv()
    a4 = [a_send(mod(z + 5, 8), 0, 1), a_send(mod(z + 3, 8), 1, 7)]
    tok_cp.wait()
    tok_x.wait_recv()
    cot_cp.wait_recv()
    for cp in b_x[2:] + b_f:
        cp.wait_recv()
    w1_x = net.send(w1, o1, partner)
    for cp in c_y[2:] + c_f:
        cp.wait_recv()
    w2_x = net.send(w2, o2, partner)

    @pl.loop(0, 4)
    def _(i):
        r = pl.ds(pl.multiple_of(i * 256, 256), 256)
        w = jnp.concatenate([w1[...].reshape(D, HD), w2[...].reshape(D, HD)], 1)
        qkv[r, 128:384] = dot(tok[r, :], w).astype(bf16)

    rows = [slice(0, 512), slice(512, 1024)]
    state = [dot(qkv[r, 128:256], qkv[r, 256:384], 0, 0) for r in rows]
    st_snd[...] = (state[0] + state[1]).astype(bf16)
    prior[0] = jnp.zeros((HD, HD), f32)
    prior[1] = state[0]
    st = [net.send_if(place(dx, dl) > here, st_snd, st_rcv.at[i], gd(dx, dl)) for i, (dx, dl) in enumerate(group)]

    for cp in a4:
        cp.wait_recv()
    w0_x = net.send(w0, o0, partner)

    @pl.loop(0, 4)
    def _(i):
        r = pl.ds(pl.multiple_of(i * 256, 256), 256)
        qkv[r, 0:128] = dot(tok[r, :], w0[...].reshape(D, HD)).astype(bf16)

    causal = lax.broadcasted_iota(jnp.int32, (512, 512), 0) >= lax.broadcasted_iota(jnp.int32, (512, 512), 1)
    for b, r in enumerate(rows):
        scores[b] = jnp.where(causal, dot(qkv[r, 0:128], qkv[r, 128:256], 1, 1), 0.0).astype(bf16)
        mixl[b] = dot(scores[b], qkv[r, 256:384])
    for i, (dx, dl) in enumerate(group):

        @pl.when(place(4 - dx, dl) < here)
        def _(i=i):
            st[i].wait_recv()
            got = st_rcv[i].astype(f32)
            prior[0] += got
            prior[1] += got

    back = []
    for b, r in enumerate(rows):
        p_hi, p_lo = split(prior[b])
        q = qkv[r, 0:128]
        mix = mixl[b] + (dot(q, p_hi) + dot(q, p_lo))
        s = lax.rsqrt(jnp.mean(mix * mix, -1, keepdims=True) + EPS)
        att_snd[b] = (mix * s).astype(bf16)
        g = cotb[b].astype(f32)
        m = jnp.mean(g * mix, -1, keepdims=True)
        dmix[b] = (s * g - s * s * s * mix * m).astype(bf16)
        back.append(dot(q, dmix[b], 0, 0))
    bk_snd[...] = (back[0] + back[1]).astype(bf16)
    later[1] = jnp.zeros((HD, HD), f32)
    later[0] = back[1]
    bk = [net.send_if(place(dx, dl) < here, bk_snd, bk_rcv.at[i], gd(dx, dl)) for i, (dx, dl) in enumerate(group)]
    att_x = net.send(att_snd.at[oc], att_oth, partner)
    att_o[:, lane_c] = att_snd[c]

    d_loc = []
    for b, r in enumerate(rows):
        q, k, v = qkv[r, 0:128], qkv[r, 128:256], qkv[r, 256:384]
        bs = jnp.where(causal, dot(dmix[b], v, 1, 1), 0.0).astype(bf16)
        p_hi, p_lo = split(prior[b])
        d_all[r, 0:128] = (dot(bs, k) + (dot(dmix[b], p_hi, 1, 1) + dot(dmix[b], p_lo, 1, 1))).astype(bf16)
        mixl[b] = dot(bs, q, 0, 0)
        d_loc.append(dot(scores[b], dmix[b], 0, 0))

    def p_q(k):
        at = mod(z + k, 8)
        cols = pl.ds(pl.multiple_of(at * 512, 512), 512)
        p0[at] = dot(tok[:, cols], d_all[:, 0:128], 0, 0).reshape(BLK[1:])

    def a_out(way, step, half, plus):
        k = 5 - step
        at = mod(z + (k if way == 0 else 8 - k), 8)
        val = p0[at, half]
        if plus is not None:
            plus.wait_recv()
            val = val + ra[way, step - 2, half].astype(f32)
        sa[way, step - 1, half] = val.astype(bf16)
        return net.send(sa.at[way, step - 1, half], ra.at[way, step - 1, half], zd(1 if way == 0 else 7))

    p_q(4)
    r1 = [a_out(0, 1, 0, None), a_out(1, 1, 1, None)]
    p_q(3)
    r2r = [None, a_out(0, 2, 1, None)]
    p_q(5)
    r2l = [a_out(1, 2, 0, None), None]
    r2r[0] = a_out(0, 2, 0, r1[0])
    r2l[1] = a_out(1, 2, 1, r1[1])
    p_q(2)
    p_q(6)
    r3r = [None, a_out(0, 3, 1, r2r[1])]
    r3l = [a_out(1, 3, 0, r2l[0]), None]
    p_q(1)
    p_q(7)
    p_q(0)

    for i, (dx, dl) in enumerate(group):

        @pl.when(place(4 - dx, dl) > here)
        def _(i=i):
            bk[i].wait_recv()
            got = bk_rcv[i].astype(f32)
            later[0] += got
            later[1] += got

    for b, r in enumerate(rows):
        l_hi, l_lo = split(later[b])
        k, v = qkv[r, 128:256], qkv[r, 256:384]
        d_all[r, 128:256] = (mixl[b] + (dot(v, l_hi, 1, 1) + dot(v, l_lo, 1, 1))).astype(bf16)
        d_all[r, 256:384] = (d_loc[b] + (dot(k, l_hi) + dot(k, l_lo))).astype(bf16)
    d_x = net.send(d_all.at[pl.ds(pl.multiple_of(oc * 512, 512), 512)], d_oth, partner)

    r3r[0] = a_out(0, 3, 0, r2r[0])
    r3l[1] = a_out(1, 3, 1, r2l[1])

    def p_kv(first):
        @pl.loop(first, first + 4)
        def _(j):
            cols = pl.ds(pl.multiple_of(j * 512, 512), 512)
            got = dot(tok[:, cols], d_all[:, 128:384], 0, 0)
            p1[j] = got[:, 0:128].reshape(BLK[1:])
            p2[j] = got[:, 128:256].reshape(BLK[1:])

    def halves(h):
        return pl.ds(4 * h, 4)

    def b_out(way, step, h, plus):
        k = 3 - step
        at = mod(x + (k if way == 0 else 4 - k), 4)
        val = p1[halves(h), :, at]
        if plus is not None:
            plus.wait_recv()
            val = val + rb[way, 0, halves(h)].astype(f32)
        sb[way, step - 1, halves(h)] = val.astype(bf16)
        return net.send(sb.at[way, step - 1, halves(h)], rb.at[way, step - 1, halves(h)], xd(1 if way == 0 else 3))

    def c_out(way, step, h, plus):
        k = 3 - step
        at = mod(y + (k if way == 0 else 4 - k), 4)
        ah, al = lax.div(at, jnp.int32(2)), mod(at, 2)
        val = p2[halves(h), ah, :, al]
        if plus is not None:
            plus.wait_recv()
            val = val + rc[way, 0, halves(h)].astype(f32)
        sc[way, step - 1, halves(h)] = val.astype(bf16)
        return net.send(sc.at[way, step - 1, halves(h)], rc.at[way, step - 1, halves(h)], yd(1 if way == 0 else 3))

    p_kv(0)
    b1r, c1r = b_out(0, 1, 0, None), c_out(0, 1, 0, None)
    b2l, c2l = [b_out(1, 2, 0, None)], [c_out(1, 2, 0, None)]
    r4 = [a_out(0, 4, 1, r3r[1]), a_out(1, 4, 0, r3l[0])]
    p_kv(4)
    b1l, c1l = b_out(1, 1, 1, None), c_out(1, 1, 1, None)
    b2r, c2r = [b_out(0, 2, 1, None)], [c_out(0, 2, 1, None)]
    r4 += [a_out(0, 4, 0, r3r[0]), a_out(1, 4, 1, r3l[1])]

    d_x.wait_recv()
    for cp in (w0_x, w1_x, w2_x):
        cp.wait_recv()
    mine = pl.ds(pl.multiple_of(c * 512, 512), 512)

    def g_t(first, last):
        @pl.loop(first, last)
        def _(j):
            w = jnp.concatenate([ref[j].reshape(512, HD) for ref in (w0, w1, w2, o0, o1, o2)], 1)
            d = jnp.concatenate([d_all[mine, :], d_oth[...]], 1)
            cols = pl.ds(pl.multiple_of(j * 512, 512), 512)
            gt_buf[:, cols] = dot(d, w, 1, 1).astype(bf16)
            pltpu.make_async_copy(gt_buf.at[:, cols], gt_hbm.at[:, cols], loc_sems.at[1 + j]).start()

    g_t(0, 2)
    b2r.append(b_out(0, 2, 0, b1r))
    c2r.append(c_out(0, 2, 0, c1r))
    b2l.append(b_out(1, 2, 1, b1l))
    c2l.append(c_out(1, 2, 1, c1l))
    g_t(2, 5)
    for cp in r4:
        cp.wait_recv()
    acc_a[...] = p0[z] + ra[0, 3].astype(f32) + ra[1, 3].astype(f32)
    a_y2 = []
    for k in (1, 2, 3):
        at = mod(y + k, 4)
        sa_y[k - 1] = acc_a[lax.div(at, jnp.int32(2)), :, mod(at, 2)].astype(bf16)
        a_y2.append(net.send(sa_y.at[k - 1], ra_y.at[k - 1], yd(k)))
    g_t(5, 8)
    for cp in b2r + b2l:
        cp.wait_recv()
    acc_b[...] = p1[:, :, x] + rb[0, 1].astype(f32) + rb[1, 1].astype(f32)
    b_y2 = []
    for k in (1, 2, 3):
        at = mod(y + k, 4)
        sb_y[k - 1] = acc_b[:, lax.div(at, jnp.int32(2)), mod(at, 2)].astype(bf16)
        b_y2.append(net.send(sb_y.at[k - 1], rb_y.at[k - 1], yd(k)))
    for cp in c2r + c2l:
        cp.wait_recv()
    acc_c[...] = p2[:, yh, :, yl] + rc[0, 1].astype(f32) + rc[1, 1].astype(f32)
    c_x2 = []
    for k in (1, 2, 3):
        sc_x[k - 1] = acc_c[:, mod(x + k, 4)].astype(bf16)
        c_x2.append(net.send(sc_x.at[k - 1], rc_x.at[k - 1], xd(k)))
    for cp in a_y2:
        cp.wait_recv()
    acc_a2[...] = acc_a[yh, :, yl] + sum(ra_y[k].astype(f32) for k in range(3))
    a_x2 = []
    for k in (1, 2, 3):
        sa_x[k - 1] = acc_a2[mod(x + k, 4)].astype(bf16)
        a_x2.append(net.send(sa_x.at[k - 1], ra_x.at[k - 1], xd(k)))
    for cp in b_y2:
        cp.wait_recv()
    acc_b2[...] = acc_b[:, yh, yl] + sum(rb_y[k].astype(f32) for k in range(3))
    b_z2 = []
    for k in range(1, 8):
        sb_z[k - 1] = acc_b2[mod(z + k, 8)].astype(bf16)
        b_z2.append(net.send(sb_z.at[k - 1], rb_z.at[k - 1], zd(k)))
    for cp in c_x2:
        cp.wait_recv()
    acc_c2[...] = acc_c[:, x] + sum(rc_x[k].astype(f32) for k in range(3))
    c_z2 = []
    for k in range(1, 8):
        sc_z[k - 1] = acc_c2[mod(z + k, 8)].astype(bf16)
        c_z2.append(net.send(sc_z.at[k - 1], rc_z.at[k - 1], zd(k)))
    for cp in a_x2:
        cp.wait_recv()
    scale = 1.0 / T_DEV
    fin[0] = ((acc_a2[x] + sum(ra_x[k].astype(f32) for k in range(3))) * scale).reshape(2, 16, HD)
    for cp in b_z2:
        cp.wait_recv()
    fin[1] = ((acc_b2[z] + sum(rb_z[k].astype(f32) for k in range(7))) * scale).reshape(2, 16, HD)
    for cp in c_z2:
        cp.wait_recv()
    fin[2] = ((acc_c2[z] + sum(rc_z[k].astype(f32) for k in range(7))) * scale).reshape(2, 16, HD)
    fin_x = net.send(fin.at[:, oc], fin_oth, partner)
    for i, o in enumerate((gq_o, gk_o, gv_o)):
        o[:, lane_c] = fin[i, c]
    att_x.wait_recv()
    att_o[:, lane_o] = att_oth[...]

    @pl.loop(0, 8)
    def _(j):
        cols = pl.ds(pl.multiple_of(j * 512, 512), 512)
        pltpu.make_async_copy(gt_buf.at[:, cols], gt_hbm.at[:, cols], loc_sems.at[1 + j]).wait()

    fin_x.wait_recv()
    for i, o in enumerate((gq_o, gk_o, gv_o)):
        o[:, lane_o] = fin_oth[i]
    net.finish()


def body(tokens, w_query, w_key, w_value, cotangent):
    vm, any_ = pl.BlockSpec(memory_space=pltpu.VMEM), pl.BlockSpec(memory_space=pl.ANY)

    def v(*shape, t=bf16):
        return pltpu.VMEM(shape, t)

    scratch = [v(1024, D)] + [v(*BLK)] * 6
    scratch += [v(1024, 384), v(2, 512, 128), v(2, 512, 512), v(2, 512, 128, t=f32), v(2, 512, 128)]
    scratch += [v(1024, 384), v(512, 384), v(512, 128), v(2, 512, 128)]
    scratch += [v(128, 128), v(7, 128, 128), v(128, 128), v(7, 128, 128), v(2, 128, 128, t=f32), v(2, 128, 128, t=f32)]
    scratch += [v(*BLK, t=f32)] * 3
    scratch += [v(2, 4, 2, 4, 2, 32, 128)] * 2 + [v(2, 2, 8, 2, 2, 32, 128)] * 2 + [v(2, 2, 8, 4, 32, 128)] * 2
    scratch += [v(2, 4, 2, 32, 128, t=f32), v(8, 2, 2, 32, 128, t=f32), v(8, 4, 32, 128, t=f32)]
    scratch += [v(3, 4, 32, 128)] * 2 + [v(3, 32, 128)] * 2 + [v(4, 32, 128, t=f32)]
    scratch += [v(3, 8, 32, 128)] * 2 + [v(7, 32, 128)] * 2 + [v(8, 32, 128, t=f32)]
    scratch += [v(3, 8, 32, 128)] * 2 + [v(7, 32, 128)] * 2 + [v(8, 32, 128, t=f32)]
    scratch += [v(3, 2, 16, 128, t=f32), v(3, 16, 128, t=f32), v(512, D)]
    scratch += [pltpu.SemaphoreType.DMA((N_SEM,)), pltpu.SemaphoreType.DMA((N_SEM,)), pltpu.SemaphoreType.DMA((9,))]
    grad = jax.ShapeDtypeStruct((16, 256), f32)
    return pl.pallas_call(
        kernel,
        out_shape=(
            jax.ShapeDtypeStruct((T_DEV, 256), bf16),
            jax.ShapeDtypeStruct((T_DEV, D), bf16),
            grad,
            grad,
            grad,
        ),
        in_specs=[any_, vm, vm, vm, vm],
        out_specs=(vm, any_, vm, vm, vm),
        scratch_shapes=scratch,
        compiler_params=pltpu.CompilerParams(collective_id=0, has_side_effects=True, vmem_limit_bytes=60 * 2**20),
        cost_estimate=pl.CostEstimate(flops=10**10, bytes_accessed=10**7, transcendentals=1024),
        name="step",
    )(tokens, w_query, w_key, w_value, cotangent)


def solution(mesh):
    both = P(("rep", "seq"), None)
    rep = P("rep", None)
    return jax.shard_map(
        body, mesh=mesh, in_specs=(both, rep, rep, rep, both), out_specs=(both,) * 5, check_vma=False
    )
```

```python
import jax
import jax.numpy as jnp
from jax import lax
from jax.experimental import pallas as pl
from jax.experimental.pallas import tpu as pltpu
from jax.sharding import PartitionSpec as P

D = 4096
HD = 128
T_DEV = 512
EPS = 1e-06
MESH = pl.DeviceIdType.MESH
f32 = jnp.float32
bf16 = jnp.bfloat16
N_SEM = 256
BLK = (8, 2, 4, 2, 32, 128)


def mod(a, n):
    return lax.rem(a, jnp.int32(n))


def dot(a, b, ca=1, cb=0):
    return lax.dot_general(a, b, (((ca,), (cb,)), ((), ())), preferred_element_type=f32)


def split(a):
    hi = a.astype(bf16)
    return hi, (a - hi.astype(f32)).astype(bf16)


class Net:
    def __init__(self, send_sems, recv_sems):
        self.ss, self.rs, self.n, self.open = send_sems, recv_sems, 0, []

    def make(self, src, dst, to):
        i = self.n
        self.n += 1
        assert i < N_SEM
        return pltpu.make_async_remote_copy(
            src_ref=src, dst_ref=dst, send_sem=self.ss.at[i], recv_sem=self.rs.at[i], device_id=to, device_id_type=MESH
        )

    def send(self, src, dst, to):
        cp = self.make(src, dst, to)
        cp.start()
        self.open.append((cp, None))
        return cp

    def send_if(self, cond, src, dst, to):
        cp = self.make(src, dst, to)
        pl.when(cond)(cp.start)
        self.open.append((cp, cond))
        return cp

    def finish(self):
        for cp, cond in self.open:
            if cond is None:
                cp.wait_send()
            else:
                pl.when(cond)(cp.wait_send)


OFF = (0, 1, 7, 2, 6, 3, 5, 4)
SLOT = {k: p for p, k in enumerate(OFF)}
GROUPS = ((0, 1), (1, 3), (3, 5), (5, 8))


def back(k):
    return (8 - k) % 8


def kernel(
    tok_hbm, wq, wk, wv, cot, att_o, gt_o, gq_o, gk_o, gv_o,
    tok, w0, w1, w2, o0, o1, o2, acc, qkv, cotb, scores, mixl, dmix, d_all, d_oth, att_oth, att_snd,
    st_snd, st_rcv, bk_snd, bk_rcv, prior, later,
    p0, p1, p2, sa, ra, sb, rb, sc, rc, acc_a, acc_b, acc_c,
    sa_y, ra_y, sa_x, ra_x, acc_a2, sb_y, rb_y, sb_z, rb_z, acc_b2, sc_x, rc_x, sc_z, rc_z, acc_c2,
    fin, fin_oth, send_sems, recv_sems, loc_sems,
):
    rep, seq = lax.axis_index("rep"), lax.axis_index("seq")
    z, yh = lax.div(rep, jnp.int32(2)), mod(rep, 2)
    x, yl, c = lax.div(seq, jnp.int32(4)), mod(lax.div(seq, jnp.int32(2)), 2), mod(seq, 2)
    y = yh * 2 + yl
    oc, oyh = 1 - c, 1 - yh

    def dev(x_, y_, z_, c_):
        return {"rep": z_ * 2 + lax.div(y_, jnp.int32(2)), "seq": x_ * 4 + mod(y_, 2) * 2 + c_}

    def xd(k):
        return dev(mod(x + k, 4), y, z, c)

    def yd(k):
        return dev(x, mod(y + k, 4), z, c)

    def zd(k):
        return dev(x, y, mod(z + k, 8), c)

    partner = dev(x, y, z, oc)
    across = dev(x, 3 - y, z, c)
    group = [(dx, dl) for dx in range(4) for dl in range(2) if dx or dl]

    def gd(dx, dl):
        return dev(mod(x + dx, 4), yh * 2 + mod(yl + dl, 2), z, c)

    def place(dx, dl):
        return mod(x + dx, 4) * 2 + mod(yl + dl, 2)

    here = x * 2 + yl
    xm, xp = mod(x + 3, 4), mod(x + 1, 4)
    ym, yp = mod(y + 3, 4), mod(y + 1, 4)
    ymh, yml, yph, ypl = lax.div(ym, jnp.int32(2)), mod(ym, 2), lax.div(yp, jnp.int32(2)), mod(yp, 2)
    lane_c = pl.ds(pl.multiple_of(c * HD, HD), HD)
    lane_o = pl.ds(pl.multiple_of(oc * HD, HD), HD)
    mine = pl.ds(pl.multiple_of(c * 512, 512), 512)

    def cols(p):
        return pl.ds(pl.multiple_of(mod(z + OFF[p], 8) * 512, 512), 512)

    peers = [partner] + [xd(k) for k in (1, 2, 3)] + [yd(k) for k in (1, 2, 3)] + [zd(k) for k in range(1, 8)]
    peers += [gd(dx, 1) for dx in (1, 2, 3)]
    bar = pltpu.get_barrier_semaphore()
    for to in peers:
        pl.semaphore_signal(bar, inc=1, device_id=to, device_id_type=MESH)
    loads = [
        pltpu.make_async_copy(src, dst, loc_sems.at[i])
        for i, (src, dst) in enumerate(
            (
                (wk.at[x, yl, :, lane_c], w1.at[0, yh, x, yl]),
                (wv.at[x, yl, :, lane_c], w2.at[0, yh, x, yl]),
                (wq.at[:, :, :, lane_c], w0.at[0, yh]),
                (tok_hbm, tok.at[mine]),
                (cot.at[:, lane_c], cotb.at[c]),
            )
        )
    ]
    for cp in loads:
        cp.start()
    for cp in loads[:3]:
        cp.wait()
    pl.semaphore_wait(bar, len(peers))

    net = Net(send_sems, recv_sems)

    b_z, c_z = {}, {}
    for k in (1, 7, 2, 6, 3, 5, 4):
        to = SLOT[back(k)]
        b_z[k] = net.send(w1.at[0, yh, x, yl], w1.at[to, yh, x, yl], zd(k))
        c_z[k] = net.send(w2.at[0, yh, x, yl], w2.at[to, yh, x, yl], zd(k))

    def a_send(half, k, way):
        at, to = (back(k), back(k + 1)) if way == 0 else (k, k + 1)
        return net.send(w0.at[SLOT[at], half], w0.at[SLOT[to], half], zd(1 if way == 0 else 7))

    def slots(g):
        return pl.ds(g[0], g[1] - g[0])

    def b_y(g):
        ref = w1.at[slots(g), yh, x, yl]
        return [net.send(ref, ref, yd(k)) for k in (1, 3, 2)]

    def c_x(g):
        ref = w2.at[slots(g), yh, x, yl]
        return [net.send(ref, ref, xd(k)) for k in (1, 3, 2)]

    def wait(cps):
        for cp in cps:
            cp.wait_recv()

    def z_wait(g):
        for p in range(*g):
            b_z[back(OFF[p])].wait_recv()
            c_z[back(OFF[p])].wait_recv()

    def b_x(g, prev):
        wait(prev)
        ref = [w1.at[slots(g), h, x] for h in (0, 1)]
        return [net.send(ref[h], ref[h], xd(k)) for h, k in ((0, 1), (1, 3), (1, 1), (0, 3))]

    def c_y(g, prev):
        wait(prev)
        ref = [w2.at[slots(g), yh, pl.ds(2 * h, 2), yl] for h in (0, 1)]
        return [net.send(ref[h], ref[h], yd(k)) for h, k in ((0, 1), (1, 3), (1, 1), (0, 3))]

    def b_f(g, prev):
        prev[0].wait_recv()
        ref = w1.at[slots(g), 0, xm]
        out = [net.send(ref, ref, xd(1))]
        prev[1].wait_recv()
        ref = w1.at[slots(g), 1, xp]
        return prev[2:] + out + [net.send(ref, ref, xd(3))]

    def c_f(g, prev):
        prev[0].wait_recv()
        ref = w2.at[slots(g), ymh, pl.ds(0, 2), yml]
        out = [net.send(ref, ref, yd(1))]
        prev[1].wait_recv()
        ref = w2.at[slots(g), yph, pl.ds(2, 2), ypl]
        return prev[2:] + out + [net.send(ref, ref, yd(3))]

    ga, gb, gc, ge = GROUPS
    b1, c1 = [b_y(ga)], [c_x(ga)]
    a_y = net.send(w0.at[0, yh], w0.at[0, yh], across)
    a1 = [a_send(yh, 0, 0), a_send(yh, 0, 1)]
    cot_x = net.send(cot.at[:, lane_o], cotb.at[c], partner)
    tok_x = net.send(tok_hbm, tok.at[mine], partner)

    def a_step(prev, k):
        out = []
        for i, half in ((0, yh), (2, oyh)):
            prev[i].wait_recv()
            out.append(a_send(half, k, 0))
            prev[i + 1].wait_recv()
            out.append(a_send(half, k, 1))
        return out

    def project(ps, lanes, ws, first):
        @pl.loop(0, 2)
        def _(i):
            r = pl.ds(pl.multiple_of(i * 512, 512), 512)
            got = None
            for p in ps:
                w = jnp.concatenate([w[p].reshape(512, HD) for w in ws], 1)
                term = dot(tok[r, cols(p)], w)
                got = term if got is None else got + term
            acc[r, lanes] = got if first else acc[r, lanes] + got

    def q_acc(*ps):
        project(ps, slice(0, 128), (w0,), ps[0] == 0)

    def kv_acc(g):
        project(range(*g), slice(128, 384), (w1, w2), g[0] == 0)

    z_wait(gb)
    b1.append(b_y(gb))
    c1.append(c_x(gb))
    a_y.wait_recv()
    a1 += [a_send(oyh, 0, 0), a_send(oyh, 0, 1)]
    b2, c2 = [b_x(ga, b1[0])], [c_y(ga, c1[0])]
    z_wait(gc)
    b1.append(b_y(gc))
    c1.append(c_x(gc))
    a2 = a_step(a1, 1)
    b2.append(b_x(gb, b1[1]))
    c2.append(c_y(gb, c1[1]))
    z_wait(ge)
    b1.append(b_y(ge))
    c1.append(c_x(ge))
    b3, c3 = [b_f(ga, b2[0])], [c_f(ga, c2[0])]
    b2.append(b_x(gc, b1[2]))
    c2.append(c_y(gc, c1[2]))
    a3 = a_step(a2, 2)
    b3.append(b_f(gb, b2[1]))
    c3.append(c_f(gb, c2[1]))
    b2.append(b_x(ge, b1[3]))
    c2.append(c_y(ge, c1[3]))
    loads[3].wait()
    tok_x.wait_recv()
    q_acc(0)
    wait(b3[0] + c3[0])
    kv_acc(ga)
    b3.append(b_f(gc, b2[2]))
    c3.append(c_f(gc, c2[2]))
    q_acc(1, 2)
    wait(a3)
    a4 = [a_send(0, 3, 0), a_send(1, 3, 1)]
    wait(b3[1] + c3[1])
    kv_acc(gb)
    q_acc(3, 4)
    b3.append(b_f(ge, b2[3]))
    c3.append(c_f(ge, c2[3]))
    wait(b3[2] + c3[2])
    kv_acc(gc)
    q_acc(5, 6)
    wait(b3[3] + c3[3])
    w_x = [net.send(w1, o1, partner), net.send(w2, o2, partner)]
    kv_acc(ge)

    rows = [slice(0, 512), slice(512, 1024)]
    state = []
    for r in rows:
        qkv[r, 128:384] = acc[r, 128:384].astype(bf16)
        state.append(dot(qkv[r, 128:256], qkv[r, 256:384], 0, 0))
    st_snd[...] = (state[0] + state[1]).astype(bf16)
    prior[0] = jnp.zeros((HD, HD), f32)
    prior[1] = state[0]
    st = [net.send_if(place(dx, dl) > here, st_snd, st_rcv.at[i], gd(dx, dl)) for i, (dx, dl) in enumerate(group)]

    wait(a4)
    w_x.append(net.send(w0, o0, partner))
    q_acc(7)
    qkv[:, 0:128] = acc[:, 0:128].astype(bf16)
    causal = lax.broadcasted_iota(jnp.int32, (512, 512), 0) >= lax.broadcasted_iota(jnp.int32, (512, 512), 1)
    for b, r in enumerate(rows):
        scores[b] = jnp.where(causal, dot(qkv[r, 0:128], qkv[r, 128:256], 1, 1), 0.0).astype(bf16)
        mixl[b] = dot(scores[b], qkv[r, 256:384])
    loads[4].wait()
    cot_x.wait_recv()
    for i, (dx, dl) in enumerate(group):

        @pl.when(place(4 - dx, dl) < here)
        def _(i=i):
            st[i].wait_recv()
            got = st_rcv[i].astype(f32)
            prior[0] += got
            prior[1] += got

    back_state = []
    for b, r in enumerate(rows):
        p_hi, p_lo = split(prior[b])
        q = qkv[r, 0:128]
        mix = mixl[b] + (dot(q, p_hi) + dot(q, p_lo))
        s = lax.rsqrt(jnp.mean(mix * mix, -1, keepdims=True) + EPS)
        att_snd[b] = (mix * s).astype(bf16)
        g = cotb[b].astype(f32)
        m = jnp.mean(g * mix, -1, keepdims=True)
        dmix[b] = (s * g - s * s * s * mix * m).astype(bf16)
        back_state.append(dot(q, dmix[b], 0, 0))
    bk_snd[...] = (back_state[0] + back_state[1]).astype(bf16)
    later[1] = jnp.zeros((HD, HD), f32)
    later[0] = back_state[1]
    bk = [net.send_if(place(dx, dl) < here, bk_snd, bk_rcv.at[i], gd(dx, dl)) for i, (dx, dl) in enumerate(group)]
    att_x = net.send(att_snd.at[oc], att_oth, partner)
    att_o[:, lane_c] = att_snd[c]

    d_loc = []
    for b, r in enumerate(rows):
        q, k, v = qkv[r, 0:128], qkv[r, 128:256], qkv[r, 256:384]
        bs = jnp.where(causal, dot(dmix[b], v, 1, 1), 0.0).astype(bf16)
        p_hi, p_lo = split(prior[b])
        d_all[r, 0:128] = (dot(bs, k) + (dot(dmix[b], p_hi, 1, 1) + dot(dmix[b], p_lo, 1, 1))).astype(bf16)
        mixl[b] = dot(bs, q, 0, 0)
        d_loc.append(dot(scores[b], dmix[b], 0, 0))

    def p_q(p):
        p0[p] = dot(tok[:, cols(p)], d_all[:, 0:128], 0, 0).reshape(BLK[1:])

    def p_kv(g):
        for p in range(*g):
            got = dot(tok[:, cols(p)], d_all[:, 128:384], 0, 0)
            p1[p] = got[:, 0:128].reshape(BLK[1:])
            p2[p] = got[:, 128:256].reshape(BLK[1:])

    def p_qkv(g):
        for p in range(*g):
            got = dot(tok[:, cols(p)], d_all[...], 0, 0)
            p0[p] = got[:, 0:128].reshape(BLK[1:])
            p1[p] = got[:, 128:256].reshape(BLK[1:])
            p2[p] = got[:, 256:384].reshape(BLK[1:])

    def a_out(way, step, half, plus):
        k = 5 - step
        val = p0[SLOT[k if way == 0 else 8 - k], half]
        if plus is not None:
            plus.wait_recv()
            val = val + ra[way, step - 2, half].astype(f32)
        sa[way, step - 1, half] = val.astype(bf16)
        return net.send(sa.at[way, step - 1, half], ra.at[way, step - 1, half], zd(1 if way == 0 else 7))

    p_q(7)
    r1 = [a_out(0, 1, 0, None), a_out(1, 1, 1, None)]
    p_q(5)
    r2r = [None, a_out(0, 2, 1, None)]
    p_q(6)
    r2l = [a_out(1, 2, 0, None), None]
    p_q(3)
    p_q(4)
    r2r[0] = a_out(0, 2, 0, r1[0])
    r2l[1] = a_out(1, 2, 1, r1[1])

    for i, (dx, dl) in enumerate(group):

        @pl.when(place(4 - dx, dl) > here)
        def _(i=i):
            bk[i].wait_recv()
            got = bk_rcv[i].astype(f32)
            later[0] += got
            later[1] += got

    for b, r in enumerate(rows):
        l_hi, l_lo = split(later[b])
        k, v = qkv[r, 128:256], qkv[r, 256:384]
        d_all[r, 128:256] = (mixl[b] + (dot(v, l_hi, 1, 1) + dot(v, l_lo, 1, 1))).astype(bf16)
        d_all[r, 256:384] = (d_loc[b] + (dot(k, l_hi) + dot(k, l_lo))).astype(bf16)
    d_x = net.send(d_all.at[pl.ds(pl.multiple_of(oc * 512, 512), 512)], d_oth, partner)

    r3r = [None, a_out(0, 3, 1, r2r[1])]
    r3l = [a_out(1, 3, 0, r2l[0]), None]

    def b_out(g, way, step, h, plus):
        k = 3 - step
        at = mod(x + (k if way == 0 else 4 - k), 4)
        val = p1[slots(g), h, at]
        if plus is not None:
            plus.wait_recv()
            val = val + rb[way, 0, slots(g), h].astype(f32)
        sb[way, step - 1, slots(g), h] = val.astype(bf16)
        return net.send(sb.at[way, step - 1, slots(g), h], rb.at[way, step - 1, slots(g), h], xd(1 if way == 0 else 3))

    def c_out(g, way, step, h, plus):
        k = 3 - step
        at = mod(y + (k if way == 0 else 4 - k), 4)
        part = pl.ds(2 * h, 2)
        val = p2[slots(g), lax.div(at, jnp.int32(2)), part, mod(at, 2)]
        if plus is not None:
            plus.wait_recv()
            val = val + rc[way, 0, slots(g), part].astype(f32)
        sc[way, step - 1, slots(g), part] = val.astype(bf16)
        return net.send(
            sc.at[way, step - 1, slots(g), part], rc.at[way, step - 1, slots(g), part], yd(1 if way == 0 else 3)
        )

    def first(g):
        return [
            [f(g, 0, 1, 0, None), f(g, 1, 1, 1, None), f(g, 0, 2, 1, None), f(g, 1, 2, 0, None)] for f in (b_out, c_out)
        ]

    def second(g, prev):
        return [
            q[2:] + [f(g, 0, 2, 0, q[0]), f(g, 1, 2, 1, q[1])] for f, q in zip((b_out, c_out), prev)
        ]

    def third(g, prev):
        wait(prev[0])
        acc_b[slots(g)] = p1[slots(g), :, x] + rb[0, 1, slots(g)].astype(f32) + rb[1, 1, slots(g)].astype(f32)
        out = [[], []]
        for k in (2, 1, 3):
            at = mod(y + k, 4)
            sb_y[k - 1, slots(g)] = acc_b[slots(g), lax.div(at, jnp.int32(2)), mod(at, 2)].astype(bf16)
            out[0].append(net.send(sb_y.at[k - 1, slots(g)], rb_y.at[k - 1, slots(g)], yd(k)))
        wait(prev[1])
        acc_c[slots(g)] = p2[slots(g), yh, :, yl] + rc[0, 1, slots(g)].astype(f32) + rc[1, 1, slots(g)].astype(f32)
        for k in (2, 1, 3):
            sc_x[k - 1, slots(g)] = acc_c[slots(g), mod(x + k, 4)].astype(bf16)
            out[1].append(net.send(sc_x.at[k - 1, slots(g)], rc_x.at[k - 1, slots(g)], xd(k)))
        return out

    b_last, c_last = [], []

    def fourth(g, prev):
        wait(prev[0])
        acc_b2[slots(g)] = acc_b[slots(g), yh, yl] + sum(rb_y[k, slots(g)].astype(f32) for k in range(3))
        wait(prev[1])
        acc_c2[slots(g)] = acc_c[slots(g), x] + sum(rc_x[k, slots(g)].astype(f32) for k in range(3))
        for p in range(*g):
            k = OFF[p]
            if k:
                to = SLOT[back(k)]
                sb_z[p] = acc_b2[p].astype(bf16)
                sc_z[p] = acc_c2[p].astype(bf16)
                b_last.append(net.send(sb_z.at[p], rb_z.at[to], zd(k)))
                c_last.append(net.send(sc_z.at[p], rc_z.at[to], zd(k)))

    p_kv(ge)
    f_e = first(ge)
    p_kv(gc)
    f_c = first(gc)
    r3r[0] = a_out(0, 3, 0, r2r[0])
    r3l[1] = a_out(1, 3, 1, r2l[1])
    p_qkv(gb)
    f_b = first(gb)
    s_e = second(ge, f_e)
    r4 = [a_out(0, 4, 1, r3r[1]), a_out(1, 4, 0, r3l[0])]
    p_qkv(ga)
    f_a = first(ga)
    s_c = second(gc, f_c)
    r4 += [a_out(0, 4, 0, r3r[0]), a_out(1, 4, 1, r3l[1])]

    def g_t(*ps):
        for p in ps:
            w = jnp.concatenate([ref[p].reshape(512, HD) for ref in (w0, w1, w2, o0, o1, o2)], 1)
            d = jnp.concatenate([d_all[mine, :], d_oth[...]], 1)
            gt_o[:, cols(p)] = dot(d, w, 1, 1).astype(bf16)

    s_b = second(gb, f_b)
    t_e = third(ge, s_e)
    s_a = second(ga, f_a)
    d_x.wait_recv()
    wait(w_x)
    g_t(0, 1)
    t_c = third(gc, s_c)
    wait(r4)
    acc_a[...] = p0[0] + ra[0, 3].astype(f32) + ra[1, 3].astype(f32)
    a_y2 = []
    for k in (2, 1, 3):
        at = mod(y + k, 4)
        sa_y[k - 1] = acc_a[lax.div(at, jnp.int32(2)), :, mod(at, 2)].astype(bf16)
        a_y2.append(net.send(sa_y.at[k - 1], ra_y.at[k - 1], yd(k)))
    fourth(ge, t_e)
    g_t(2, 3)
    t_b = third(gb, s_b)
    fourth(gc, t_c)
    wait(a_y2)
    acc_a2[...] = acc_a[yh, :, yl] + sum(ra_y[k].astype(f32) for k in range(3))
    a_x2 = []
    for k in (2, 1, 3):
        sa_x[k - 1] = acc_a2[mod(x + k, 4)].astype(bf16)
        a_x2.append(net.send(sa_x.at[k - 1], ra_x.at[k - 1], xd(k)))
    t_a = third(ga, s_a)
    g_t(4, 5)
    fourth(gb, t_b)
    g_t(6, 7)
    att_x.wait_recv()
    att_o[:, lane_o] = att_oth[...]
    wait(a_x2)
    scale = 1.0 / T_DEV
    fin[0] = ((acc_a2[x] + sum(ra_x[k].astype(f32) for k in range(3))) * scale).reshape(2, 16, HD)
    fourth(ga, t_a)
    wait(b_last)
    fin[1] = ((acc_b2[0] + sum(rb_z[k].astype(f32) for k in range(1, 8))) * scale).reshape(2, 16, HD)
    wait(c_last)
    fin[2] = ((acc_c2[0] + sum(rc_z[k].astype(f32) for k in range(1, 8))) * scale).reshape(2, 16, HD)
    fin_x = net.send(fin.at[:, oc], fin_oth, partner)
    for i, o in enumerate((gq_o, gk_o, gv_o)):
        o[:, lane_c] = fin[i, c]
    fin_x.wait_recv()
    for i, o in enumerate((gq_o, gk_o, gv_o)):
        o[:, lane_o] = fin_oth[i]
    net.finish()


def write_out(*refs):
    sems = refs[10]
    copies = [pltpu.make_async_copy(refs[i], refs[5 + i], sems.at[i]) for i in (1, 0, 2, 3, 4)]
    for cp in copies:
        cp.start()
    for cp in copies:
        cp.wait()


def body(tokens, w_query, w_key, w_value, cotangent):
    vm, any_ = pl.BlockSpec(memory_space=pltpu.VMEM), pl.BlockSpec(memory_space=pl.ANY)
    hbm = pl.BlockSpec(memory_space=pltpu.HBM)

    def v(*shape, t=bf16):
        return pltpu.VMEM(shape, t)

    scratch = [v(1024, D)] + [v(*BLK)] * 6
    scratch += [v(1024, 384, t=f32), v(1024, 384), v(2, 512, 128), v(2, 512, 512), v(2, 512, 128, t=f32), v(2, 512, 128)]
    scratch += [v(1024, 384), v(512, 384), v(512, 128), v(2, 512, 128)]
    scratch += [v(128, 128), v(7, 128, 128), v(128, 128), v(7, 128, 128), v(2, 128, 128, t=f32), v(2, 128, 128, t=f32)]
    scratch += [v(*BLK, t=f32)] * 3
    scratch += [v(2, 4, 2, 4, 2, 32, 128)] * 2 + [v(2, 2, 8, 2, 2, 32, 128)] * 2 + [v(2, 2, 8, 4, 32, 128)] * 2
    scratch += [v(2, 4, 2, 32, 128, t=f32), v(8, 2, 2, 32, 128, t=f32), v(8, 4, 32, 128, t=f32)]
    scratch += [v(3, 4, 32, 128)] * 2 + [v(3, 32, 128)] * 2 + [v(4, 32, 128, t=f32)]
    scratch += [v(3, 8, 32, 128)] * 2 + [v(8, 32, 128)] * 2 + [v(8, 32, 128, t=f32)]
    scratch += [v(3, 8, 32, 128)] * 2 + [v(8, 32, 128)] * 2 + [v(8, 32, 128, t=f32)]
    scratch += [v(3, 2, 16, 128, t=f32), v(3, 16, 128, t=f32)]
    scratch += [pltpu.SemaphoreType.DMA((N_SEM,)), pltpu.SemaphoreType.DMA((N_SEM,)), pltpu.SemaphoreType.DMA((5,))]
    grad = pltpu.VMEM((16, 256), f32)
    args = [tokens] + [w.reshape(4, 2, 32, 256) for w in (w_query, w_key, w_value)] + [cotangent]
    outs = pl.pallas_call(
        kernel,
        out_shape=(
            pltpu.VMEM((T_DEV, 256), bf16),
            pltpu.VMEM((T_DEV, D), bf16),
            grad,
            grad,
            grad,
        ),
        in_specs=[hbm] * 5,
        out_specs=(vm, vm, vm, vm, vm),
        scratch_shapes=scratch,
        compiler_params=pltpu.CompilerParams(collective_id=0, has_side_effects=True, vmem_limit_bytes=48 * 2**20),
        cost_estimate=pl.CostEstimate(flops=10**10, bytes_accessed=10**7, transcendentals=1024),
        name="step",
    )(*[pltpu.with_memory_space_constraint(a, pltpu.HBM) for a in args])
    return pl.pallas_call(
        write_out,
        out_shape=[jax.ShapeDtypeStruct(o.shape, o.dtype) for o in outs],
        in_specs=[vm] * 5,
        out_specs=[any_] * 5,
        scratch_shapes=[pltpu.SemaphoreType.DMA((5,))],
        compiler_params=pltpu.CompilerParams(vmem_limit_bytes=2**20),
        name="write_out",
    )(*[pltpu.with_memory_space_constraint(o, pltpu.VMEM) for o in outs])


def solution(mesh):
    both = P(("rep", "seq"), None)
    rep = P("rep", None)
    return jax.shard_map(
        body, mesh=mesh, in_specs=(both, rep, rep, rep, both), out_specs=(both,) * 5, check_vma=False
    )
```

```python
import math

import jax
import jax.numpy as jnp
from jax import lax
from jax.experimental import pallas as pl
from jax.experimental.pallas import tpu as pltpu
from jax.sharding import PartitionSpec as P

D = 4096
HD = 128
T_DEV = 512
EPS = 1e-06
MESH = pl.DeviceIdType.MESH
f32 = jnp.float32
bf16 = jnp.bfloat16
N_SEM = 64
BLK = (8, 2, 4, 2, 32, 128)


def mod(a, n):
    return lax.rem(a, jnp.int32(n))


def dot(a, b, ca=1, cb=0):
    return lax.dot_general(a, b, (((ca,), (cb,)), ((), ())), preferred_element_type=f32)


def split(a):
    hi = a.astype(bf16)
    return hi, (a - hi.astype(f32)).astype(bf16)


class Batch:
    def __init__(self, net):
        self.net, self.i, self.copies, self.units = net, net.n, [], 0
        net.n += 1
        assert net.n <= N_SEM
        net.batches.append(self)

    def send(self, src, dst, to):
        cp = self.net.make(src, dst, to, self.i)
        cp.start()
        self.copies.append(cp)
        self.units += math.prod(src.shape) // 2048

    def all(self):
        if len(self.copies) == 1:
            return self.copies[0]
        ref = self.net.sizes.at[pl.ds(0, self.units)]
        return self.net.make(ref, ref, self.net.anyone, self.i)

    def wait(self):
        self.all().wait_recv()


class Net:
    def __init__(self, send_sems, recv_sems, sizes, anyone):
        self.ss, self.rs, self.sizes, self.anyone = send_sems, recv_sems, sizes, anyone
        self.n, self.batches, self.maybe = 0, [], []

    def make(self, src, dst, to, i):
        return pltpu.make_async_remote_copy(
            src_ref=src, dst_ref=dst, send_sem=self.ss.at[i], recv_sem=self.rs.at[i], device_id=to, device_id_type=MESH
        )

    def one(self, src, dst, to):
        b = Batch(self)
        b.send(src, dst, to)
        return b

    def some(self, sends):
        b = Batch(self)
        for src, dst, to in sends:
            b.send(src, dst, to)
        return b

    def send_if(self, cond, src, dst, to, i):
        cp = self.make(src, dst, to, i)
        pl.when(cond)(cp.start)
        self.maybe.append((cp, cond))
        return cp

    def finish(self):
        for b in self.batches:
            b.all().wait_send()
        for cp, cond in self.maybe:
            pl.when(cond)(cp.wait_send)


OFF = (0, 1, 7, 2, 6, 3, 5, 4)
SLOT = {k: p for p, k in enumerate(OFF)}
GROUPS = ((0, 1), (1, 3), (3, 5), (5, 8))


def back(k):
    return (8 - k) % 8


def kernel(
    tok_hbm, wq, wk, wv, cot, att_o, gt_o, gq_o, gk_o, gv_o,
    tok, w0, w1, w2, o0, o1, o2, acc, qkv, cotb, scores, mixl, d_loc, dmix, d_all, d_oth, att_oth, att_snd,
    st_snd, st_rcv, bk_snd, bk_rcv, prior, later,
    p0, p1, p2, sa, ra, acc_a, acc_b, acc_c,
    sa_y, ra_y, sa_x, ra_x, acc_a2, sb_y, rb_y, sb_z, rb_z, acc_b2, sc_x, rc_x, sc_z, rc_z, acc_c2,
    sb_d, rb_d, sc_d, rc_d, sizes, send_sems, recv_sems, loc_sems,
):
    rep, seq = lax.axis_index("rep"), lax.axis_index("seq")
    z, yh = lax.div(rep, jnp.int32(2)), mod(rep, 2)
    x, yl, c = lax.div(seq, jnp.int32(4)), mod(lax.div(seq, jnp.int32(2)), 2), mod(seq, 2)
    y = yh * 2 + yl
    oc, oyh = 1 - c, 1 - yh

    def dev(x_, y_, z_, c_):
        return {"rep": z_ * 2 + lax.div(y_, jnp.int32(2)), "seq": x_ * 4 + mod(y_, 2) * 2 + c_}

    def xd(k):
        return dev(mod(x + k, 4), y, z, c)

    def yd(k):
        return dev(x, mod(y + k, 4), z, c)

    def zd(k):
        return dev(x, y, mod(z + k, 8), c)

    partner = dev(x, y, z, oc)
    across = dev(x, 3 - y, z, c)
    group = [(dx, dl) for dx in range(4) for dl in range(2) if dx or dl]

    def gd(dx, dl):
        return dev(mod(x + dx, 4), yh * 2 + mod(yl + dl, 2), z, c)

    def place(dx, dl):
        return mod(x + dx, 4) * 2 + mod(yl + dl, 2)

    here = x * 2 + yl
    xm, xp = mod(x + 3, 4), mod(x + 1, 4)
    ym, yp = mod(y + 3, 4), mod(y + 1, 4)
    ymh, yml, yph, ypl = lax.div(ym, jnp.int32(2)), mod(ym, 2), lax.div(yp, jnp.int32(2)), mod(yp, 2)
    lane_c = pl.ds(pl.multiple_of(c * HD, HD), HD)
    lane_o = pl.ds(pl.multiple_of(oc * HD, HD), HD)
    mine = pl.ds(pl.multiple_of(c * 512, 512), 512)

    def cols(p):
        return pl.ds(pl.multiple_of(mod(z + OFF[p], 8) * 512, 512), 512)

    peers = [partner] + [xd(k) for k in (1, 2, 3)] + [yd(k) for k in (1, 2, 3)] + [zd(k) for k in range(1, 8)]
    peers += [gd(dx, 1) for dx in (1, 2, 3)]
    peers += [dev(mod(x + k, 4), y, z, oc) for k in (1, 2, 3)] + [dev(x, y, mod(z + k, 8), oc) for k in range(1, 8)]
    bar = pltpu.get_barrier_semaphore()
    for to in peers:
        pl.semaphore_signal(bar, inc=1, device_id=to, device_id_type=MESH)
    loads = [
        pltpu.make_async_copy(src, dst, loc_sems.at[i])
        for i, (src, dst) in enumerate(
            (
                (wk.at[x, yl, :, lane_c], w1.at[0, yh, x, yl]),
                (wv.at[x, yl, :, lane_c], w2.at[0, yh, x, yl]),
                (wq.at[:, :, :, lane_c], w0.at[0, yh]),
                (tok_hbm, tok.at[mine]),
                (cot.at[:, lane_c], cotb.at[c]),
            )
        )
    ]
    for cp in loads:
        cp.start()
    for cp in loads[:3]:
        cp.wait()
    pl.semaphore_wait(bar, len(peers))

    net = Net(send_sems, recv_sems, sizes, partner)

    ga, gb, gc, ge = GROUPS
    steps = {g: Batch(net) for g in GROUPS[1:]}
    for k in (1, 7, 2, 6, 3, 5, 4):
        to = SLOT[back(k)]
        for g in GROUPS[1:]:
            if to in range(*g):
                for w in (w1, w2):
                    steps[g].send(w.at[0, yh, x, yl], w.at[to, yh, x, yl], zd(k))

    def slots(g):
        return pl.ds(g[0], g[1] - g[0])

    def mid(g):
        if g in steps:
            steps[g].wait()
        b, c_ = w1.at[slots(g), yh, x, yl], w2.at[slots(g), yh, x, yl]
        return net.some([t for k in (1, 3, 2) for t in ((b, b, yd(k)), (c_, c_, xd(k)))])

    def wide(g, prev):
        prev.wait()
        b = [w1.at[slots(g), h, x] for h in (0, 1)]
        c_ = [w2.at[slots(g), yh, pl.ds(2 * h, 2), yl] for h in (0, 1)]
        lead = net.some([t for h, k in ((0, 1), (1, 3)) for t in ((b[h], b[h], xd(k)), (c_[h], c_[h], yd(k)))])
        rest = net.some([t for h, k in ((1, 1), (0, 3)) for t in ((b[h], b[h], xd(k)), (c_[h], c_[h], yd(k)))])
        return lead, rest

    def pass_on(g, prev):
        lead, rest = prev
        lead.wait()
        for ref, to in (
            (w1.at[slots(g), 0, xm], xd(1)),
            (w1.at[slots(g), 1, xp], xd(3)),
            (w2.at[slots(g), ymh, pl.ds(0, 2), yml], yd(1)),
            (w2.at[slots(g), yph, pl.ds(2, 2), ypl], yd(3)),
        ):
            rest.send(ref, ref, to)
        return rest

    def a_send(k, *parts):
        sends = []
        for half, way in parts:
            at, to = (back(k), back(k + 1)) if way == 0 else (k, k + 1)
            sends.append((w0.at[SLOT[at], half], w0.at[SLOT[to], half], zd(1 if way == 0 else 7)))
        return net.some(sends)

    def a_half(prev, half, k):
        prev.wait()
        return a_send(k, (half, 0), (half, 1))

    m_a = mid(ga)
    a_y = net.one(w0.at[0, yh], w0.at[0, yh], across)
    a1 = [a_send(0, (yh, 0), (yh, 1))]
    cot_x = net.one(cot.at[:, lane_o], cotb.at[c], partner)
    tok_x = net.one(tok_hbm, tok.at[mine], partner)

    def project(ps, lanes, ws, first):
        @pl.loop(0, 2)
        def _(i):
            r = pl.ds(pl.multiple_of(i * 512, 512), 512)
            got = None
            for p in ps:
                w = jnp.concatenate([w[p].reshape(512, HD) for w in ws], 1)
                term = dot(tok[r, cols(p)], w)
                got = term if got is None else got + term
            acc[r, lanes] = got if first else acc[r, lanes] + got

    def q_acc(*ps):
        project(ps, slice(0, 128), (w0,), ps[0] == 0)

    def kv_acc(g):
        project(range(*g), slice(128, 384), (w1, w2), g[0] == 0)

    m_b = mid(gb)
    n_a = wide(ga, m_a)
    a_y.wait()
    a1.append(a_send(0, (oyh, 0), (oyh, 1)))
    m_c = mid(gc)
    m_e = mid(ge)
    n_b = wide(gb, m_b)
    a2 = [a_half(a1[0], yh, 1)]
    f_a = pass_on(ga, n_a)
    n_c = wide(gc, m_c)
    a2.append(a_half(a1[1], oyh, 1))
    n_e = wide(ge, m_e)
    f_b = pass_on(gb, n_b)
    loads[3].wait()
    tok_x.wait()
    f_a.wait()
    kv_acc(ga)
    f_c = pass_on(gc, n_c)
    a3 = [a_half(a2[0], yh, 2)]
    q_acc(0)
    q_acc(1, 2)
    f_e = pass_on(ge, n_e)
    a3.append(a_half(a2[1], oyh, 2))
    f_b.wait()
    kv_acc(gb)
    f_c.wait()
    kv_acc(gc)
    for cp in a3:
        cp.wait()
    a4 = a_send(3, (0, 0), (1, 1))
    f_e.wait()
    w_x = [net.one(w1, o1, partner), net.one(w2, o2, partner)]
    kv_acc(ge)

    rows = [slice(0, 512), slice(512, 1024)]
    state = []
    for r in rows:
        qkv[r, 128:384] = acc[r, 128:384].astype(bf16)
        state.append(dot(qkv[r, 128:256], qkv[r, 256:384], 0, 0))
    st_snd[...] = (state[0] + state[1]).astype(bf16)
    prior[0] = jnp.zeros((HD, HD), f32)
    prior[1] = state[0]
    pair = net.n
    net.n += len(group)
    st = [
        net.send_if(place(dx, dl) > here, st_snd, st_rcv.at[i], gd(dx, dl), pair + i) for i, (dx, dl) in enumerate(group)
    ]

    q_acc(3, 4, 5, 6)
    a4.wait()
    w_x.append(net.one(w0, o0, partner))
    q_acc(7)
    qkv[:, 0:128] = acc[:, 0:128].astype(bf16)
    causal = lax.broadcasted_iota(jnp.int32, (512, 512), 0) >= lax.broadcasted_iota(jnp.int32, (512, 512), 1)
    for b, r in enumerate(rows):
        scores[b] = jnp.where(causal, dot(qkv[r, 0:128], qkv[r, 128:256], 1, 1), 0.0).astype(bf16)
        mixl[b] = dot(scores[b], qkv[r, 256:384])
    loads[4].wait()
    cot_x.wait()
    for i, (dx, dl) in enumerate(group):

        @pl.when(place(4 - dx, dl) < here)
        def _(i=i):
            st[i].wait_recv()
            got = st_rcv[i].astype(f32)
            prior[0] += got
            prior[1] += got

    back_state = []
    for b, r in enumerate(rows):
        p_hi, p_lo = split(prior[b])
        q = qkv[r, 0:128]
        mix = mixl[b] + (dot(q, p_hi) + dot(q, p_lo))
        s = lax.rsqrt(jnp.mean(mix * mix, -1, keepdims=True) + EPS)
        att_snd[b] = (mix * s).astype(bf16)
        g = cotb[b].astype(f32)
        m = jnp.mean(g * mix, -1, keepdims=True)
        dmix[b] = (s * g - s * s * s * mix * m).astype(bf16)
        back_state.append(dot(q, dmix[b], 0, 0))
    bk_snd[...] = (back_state[0] + back_state[1]).astype(bf16)
    later[1] = jnp.zeros((HD, HD), f32)
    later[0] = back_state[1]
    bk = [
        net.send_if(place(dx, dl) < here, bk_snd, bk_rcv.at[i], gd(dx, dl), pair + i) for i, (dx, dl) in enumerate(group)
    ]
    att_x = net.one(att_snd.at[oc], att_oth, partner)

    for b, r in enumerate(rows):
        q, k, v = qkv[r, 0:128], qkv[r, 128:256], qkv[r, 256:384]
        bs = jnp.where(causal, dot(dmix[b], v, 1, 1), 0.0).astype(bf16)
        p_hi, p_lo = split(prior[b])
        d_all[r, 0:128] = (dot(bs, k) + (dot(dmix[b], p_hi, 1, 1) + dot(dmix[b], p_lo, 1, 1))).astype(bf16)
        mixl[b] = dot(bs, q, 0, 0)
        d_loc[b] = dot(scores[b], dmix[b], 0, 0)

    def p_q(p):
        p0[p] = dot(tok[:, cols(p)], d_all[:, 0:128], 0, 0).reshape(BLK[1:])

    def p_kv(g):
        for p in range(*g):
            got = dot(tok[:, cols(p)], d_all[:, 128:384], 0, 0)
            p1[p] = got[:, 0:128].reshape(BLK[1:])
            p2[p] = got[:, 128:256].reshape(BLK[1:])

    def p_qkv(g):
        for p in range(*g):
            got = dot(tok[:, cols(p)], d_all[...], 0, 0)
            p0[p] = got[:, 0:128].reshape(BLK[1:])
            p1[p] = got[:, 128:256].reshape(BLK[1:])
            p2[p] = got[:, 256:384].reshape(BLK[1:])

    def a_out(step, parts, plus=None):
        if plus is not None:
            plus.wait()
        sends = []
        for way, half in parts:
            k = 5 - step
            val = p0[SLOT[k if way == 0 else 8 - k], half]
            if plus is not None:
                val = val + ra[way, step - 2, half].astype(f32)
            sa[way, step - 1, half] = val.astype(bf16)
            sends.append((sa.at[way, step - 1, half], ra.at[way, step - 1, half], zd(1 if way == 0 else 7)))
        return net.some(sends)

    ends, free = ((0, 0), (1, 1)), ((0, 1), (1, 0))
    p_q(7)
    r1 = a_out(1, ends)
    p_q(5)
    p_q(6)
    r2f = a_out(2, free)

    for i, (dx, dl) in enumerate(group):

        @pl.when(place(4 - dx, dl) > here)
        def _(i=i):
            bk[i].wait_recv()
            got = bk_rcv[i].astype(f32)
            later[0] += got
            later[1] += got

    for b, r in enumerate(rows):
        l_hi, l_lo = split(later[b])
        k, v = qkv[r, 128:256], qkv[r, 256:384]
        d_all[r, 128:256] = (mixl[b] + (dot(v, l_hi, 1, 1) + dot(v, l_lo, 1, 1))).astype(bf16)
        d_all[r, 256:384] = (d_loc[b] + (dot(k, l_hi) + dot(k, l_lo))).astype(bf16)
    d_x = net.one(d_all.at[pl.ds(pl.multiple_of(oc * 512, 512), 512)], d_oth, partner)

    def direct(g):
        out = Batch(net)
        for k in (2, 1, 3):
            sb_d[k - 1, slots(g)] = p1[slots(g), :, mod(x + k, 4)].astype(bf16)
            out.send(sb_d.at[k - 1, slots(g)], rb_d.at[k - 1, slots(g)], xd(k))
            at = mod(y + k, 4)
            sc_d[k - 1, slots(g)] = p2[slots(g), lax.div(at, jnp.int32(2)), :, mod(at, 2)].astype(bf16)
            out.send(sc_d.at[k - 1, slots(g)], rc_d.at[k - 1, slots(g)], yd(k))
        return out

    def third(g, prev):
        prev.wait()
        acc_b[slots(g)] = p1[slots(g), :, x] + sum(rb_d[k, slots(g)].astype(f32) for k in range(3))
        acc_c[slots(g)] = p2[slots(g), yh, :, yl] + sum(rc_d[k, slots(g)].astype(f32) for k in range(3))
        out = Batch(net)
        for k in (2, 1, 3):
            at = mod(y + k, 4)
            sb_y[k - 1, slots(g)] = acc_b[slots(g), lax.div(at, jnp.int32(2)), mod(at, 2)].astype(bf16)
            out.send(sb_y.at[k - 1, slots(g)], rb_y.at[k - 1, slots(g)], yd(k))
            sc_x[k - 1, slots(g)] = acc_c[slots(g), mod(x + k, 4)].astype(bf16)
            out.send(sc_x.at[k - 1, slots(g)], rc_x.at[k - 1, slots(g)], xd(k))
        return out

    last = Batch(net)

    def fourth(g, prev):
        prev.wait()
        n = g[1] - g[0]
        got = acc_b[slots(g), yh, yl] + sum(rb_y[k, slots(g)].astype(f32) for k in range(3))
        acc_b2[slots(g)] = got.reshape(n, 2, 16, HD)
        got = acc_c[slots(g), x] + sum(rc_x[k, slots(g)].astype(f32) for k in range(3))
        acc_c2[slots(g)] = got.reshape(n, 2, 16, HD)
        for snd, rcv, total in ((sb_z, rb_z, acc_b2), (sc_z, rc_z, acc_c2)):
            snd[slots(g)] = total[slots(g)].astype(bf16)
            for p in range(*g):
                k = OFF[p]
                to = SLOT[back(k)]
                if k:
                    last.send(snd.at[p, c], rcv.at[0, to], zd(k))
                last.send(snd.at[p, oc], rcv.at[1, to], dev(x, y, mod(z + k, 8), oc) if k else partner)

    def g_t(*ps):
        for p in ps:
            w = jnp.concatenate([ref[p].reshape(512, HD) for ref in (w0, w1, w2, o0, o1, o2)], 1)
            d = jnp.concatenate([d_all[mine, :], d_oth[...]], 1)
            gt_o[:, cols(p)] = dot(d, w, 1, 1).astype(bf16)

    r2 = a_out(2, ends, r1)
    p_kv(ge)
    d_e = direct(ge)
    p_qkv(gc)
    d_c = direct(gc)
    r3f = a_out(3, free, r2f)
    r3 = a_out(3, ends, r2)
    p_qkv(gb)
    d_b = direct(gb)
    p_qkv(ga)
    d_a = direct(ga)
    d_x.wait()
    for cp in w_x:
        cp.wait()
    g_t(0)
    r4f = a_out(4, free, r3f)
    r4 = a_out(4, ends, r3)
    g_t(1, 2)
    t_e = third(ge, d_e)
    t_c = third(gc, d_c)
    g_t(3)
    t_b = third(gb, d_b)
    r4f.wait()
    r4.wait()
    acc_a[...] = p0[0] + ra[0, 3].astype(f32) + ra[1, 3].astype(f32)
    a_y2 = Batch(net)
    for k in (2, 1, 3):
        at = mod(y + k, 4)
        sa_y[k - 1] = acc_a[lax.div(at, jnp.int32(2)), :, mod(at, 2)].astype(bf16)
        a_y2.send(sa_y.at[k - 1], ra_y.at[k - 1], yd(k))
    t_a = third(ga, d_a)
    fourth(ge, t_e)
    g_t(4)
    fourth(gc, t_c)
    fourth(gb, t_b)
    a_y2.wait()
    acc_a2[...] = (acc_a[yh, :, yl] + sum(ra_y[k].astype(f32) for k in range(3))).reshape(4, 2, 16, HD)
    sa_x[...] = acc_a2[...].astype(bf16)
    last.send(sa_x.at[x, oc], ra_x.at[1, 0], partner)
    for k in (2, 1, 3):
        at = mod(x + k, 4)
        last.send(sa_x.at[at, c], ra_x.at[0, k], xd(k))
        last.send(sa_x.at[at, oc], ra_x.at[1, k], dev(at, y, z, oc))
    fourth(ga, t_a)
    g_t(5, 6, 7)
    att_o[:, lane_c] = att_snd[c]
    att_x.wait()
    att_o[:, lane_o] = att_oth[...]
    scale = 1.0 / T_DEV
    last.wait()
    gq_o[:, lane_c] = (acc_a2[x, c] + sum(ra_x[0, k].astype(f32) for k in range(1, 4))) * scale
    gq_o[:, lane_o] = sum(ra_x[1, k].astype(f32) for k in range(4)) * scale
    for out, total, rcv in ((gk_o, acc_b2, rb_z), (gv_o, acc_c2, rc_z)):
        out[:, lane_c] = (total[0, c] + sum(rcv[0, p].astype(f32) for p in range(1, 8))) * scale
        out[:, lane_o] = sum(rcv[1, p].astype(f32) for p in range(8)) * scale
    net.finish()


def write_out(*refs):
    sems = refs[10]
    copies = [pltpu.make_async_copy(refs[i], refs[5 + i], sems.at[i]) for i in (1, 0, 2, 3, 4)]
    for cp in copies:
        cp.start()
    for cp in copies:
        cp.wait()


def body(tokens, w_query, w_key, w_value, cotangent):
    vm, any_ = pl.BlockSpec(memory_space=pltpu.VMEM), pl.BlockSpec(memory_space=pl.ANY)
    hbm = pl.BlockSpec(memory_space=pltpu.HBM)

    def v(*shape, t=bf16):
        return pltpu.VMEM(shape, t)

    scratch = [v(1024, D)] + [v(*BLK)] * 6
    scratch += [v(1024, 384, t=f32), v(1024, 384), v(2, 512, 128), v(2, 512, 512), v(2, 512, 128, t=f32), v(2, 512, 128, t=f32), v(2, 512, 128)]
    scratch += [v(1024, 384), v(512, 384), v(512, 128), v(2, 512, 128)]
    scratch += [v(128, 128), v(7, 128, 128), v(128, 128), v(7, 128, 128), v(2, 128, 128, t=f32), v(2, 128, 128, t=f32)]
    scratch += [v(*BLK, t=f32)] * 3
    scratch += [v(2, 4, 2, 4, 2, 32, 128)] * 2
    scratch += [v(2, 4, 2, 32, 128, t=f32), v(8, 2, 2, 32, 128, t=f32), v(8, 4, 32, 128, t=f32)]
    scratch += [v(3, 4, 32, 128)] * 2 + [v(4, 2, 16, 128), v(2, 4, 16, 128)] + [v(4, 2, 16, 128, t=f32)]
    scratch += [v(3, 8, 32, 128)] * 2 + [v(8, 2, 16, 128), v(2, 8, 16, 128)] + [v(8, 2, 16, 128, t=f32)]
    scratch += [v(3, 8, 32, 128)] * 2 + [v(8, 2, 16, 128), v(2, 8, 16, 128)] + [v(8, 2, 16, 128, t=f32)]
    scratch += [v(3, 8, 2, 2, 32, 128)] * 2 + [v(3, 8, 4, 32, 128)] * 2 + [v(160, 16, 128)]
    scratch += [pltpu.SemaphoreType.DMA((N_SEM,)), pltpu.SemaphoreType.DMA((N_SEM,)), pltpu.SemaphoreType.DMA((5,))]
    grad = pltpu.VMEM((16, 256), f32)
    args = [tokens] + [w.reshape(4, 2, 32, 256) for w in (w_query, w_key, w_value)] + [cotangent]
    outs = pl.pallas_call(
        kernel,
        out_shape=(
            pltpu.VMEM((T_DEV, 256), bf16),
            pltpu.VMEM((T_DEV, D), bf16),
            grad,
            grad,
            grad,
        ),
        in_specs=[hbm] * 5,
        out_specs=(vm, vm, vm, vm, vm),
        scratch_shapes=scratch,
        compiler_params=pltpu.CompilerParams(collective_id=0, has_side_effects=True, vmem_limit_bytes=48 * 2**20),
        cost_estimate=pl.CostEstimate(flops=10**10, bytes_accessed=10**7, transcendentals=1024),
        name="step",
    )(*[pltpu.with_memory_space_constraint(a, pltpu.HBM) for a in args])
    return pl.pallas_call(
        write_out,
        out_shape=[jax.ShapeDtypeStruct(o.shape, o.dtype) for o in outs],
        in_specs=[vm] * 5,
        out_specs=[any_] * 5,
        scratch_shapes=[pltpu.SemaphoreType.DMA((5,))],
        compiler_params=pltpu.CompilerParams(vmem_limit_bytes=2**20),
        name="write_out",
    )(*[pltpu.with_memory_space_constraint(o, pltpu.VMEM) for o in outs])


def solution(mesh):
    both = P(("rep", "seq"), None)
    rep = P("rep", None)
    return jax.shard_map(
        body, mesh=mesh, in_specs=(both, rep, rep, rep, both), out_specs=(both,) * 5, check_vma=False
    )
```

```python
import math

import jax
import jax.numpy as jnp
from jax import lax
from jax.experimental import pallas as pl
from jax.experimental.pallas import tpu as pltpu
from jax.sharding import PartitionSpec as P

D = 4096
HD = 128
T_DEV = 512
EPS = 1e-06
MESH = pl.DeviceIdType.MESH
f32 = jnp.float32
bf16 = jnp.bfloat16
N_SEM = 53
BLK = (8, 2, 4, 2, 32, 128)


def mod(a, n):
    return lax.rem(a, jnp.int32(n))


def dot(a, b, ca=1, cb=0):
    return lax.dot_general(a, b, (((ca,), (cb,)), ((), ())), preferred_element_type=f32)


def split(a):
    hi = a.astype(bf16)
    return hi, (a - hi.astype(f32)).astype(bf16)


class Batch:
    def __init__(self, net):
        self.net, self.i, self.copies, self.units = net, net.n, [], 0
        net.n += 1
        assert net.n <= N_SEM
        net.batches.append(self)

    def send(self, src, dst, to):
        cp = self.net.make(src, dst, to, self.i)
        cp.start()
        self.copies.append(cp)
        self.units += math.prod(src.shape) // 2048

    def all(self):
        if len(self.copies) == 1:
            return self.copies[0]
        ref = self.net.sizes.at[pl.ds(0, self.units)]
        return self.net.make(ref, ref, self.net.anyone, self.i)

    def wait(self):
        self.all().wait_recv()


class Net:
    def __init__(self, send_sems, recv_sems, sizes, anyone):
        self.ss, self.rs, self.sizes, self.anyone = send_sems, recv_sems, sizes, anyone
        self.n, self.batches, self.maybe = 0, [], []

    def make(self, src, dst, to, i):
        return pltpu.make_async_remote_copy(
            src_ref=src, dst_ref=dst, send_sem=self.ss.at[i], recv_sem=self.rs.at[i], device_id=to, device_id_type=MESH
        )

    def one(self, src, dst, to):
        b = Batch(self)
        b.send(src, dst, to)
        return b

    def some(self, sends):
        b = Batch(self)
        for src, dst, to in sends:
            b.send(src, dst, to)
        return b

    def send_if(self, cond, src, dst, to, i):
        cp = self.make(src, dst, to, i)
        pl.when(cond)(cp.start)
        self.maybe.append((cp, cond))
        return cp

    def finish(self):
        for b in self.batches:
            b.all().wait_send()
        for cp, cond in self.maybe:
            pl.when(cond)(cp.wait_send)


OFF = (0, 1, 7, 2, 6, 3, 5, 4)
SLOT = {k: p for p, k in enumerate(OFF)}
GROUPS = ((0, 1), (1, 3), (3, 5), (5, 8))


def back(k):
    return (8 - k) % 8


def kernel(
    tok_hbm, wq, wk, wv, cot, att_o, gt_o, gq_o, gk_o, gv_o,
    tok, w0, w1, w2, o0, o1, o2, acc, qkv, cotb, scores, mixl, d_loc, dmix, d_all, d_oth, att_oth, att_snd,
    st_snd, st_rcv, bk_snd, bk_rcv, prior, later,
    p0, p1, p2, sa, ra, acc_a, acc_b, acc_c,
    sa_x, ra_x, sb_y, rb_y, sb_z, rb_z, acc_b2, sc_x, rc_x, sc_z, rc_z, acc_c2,
    sb_d, rb_d, sc_d, rc_d, sizes, send_sems, recv_sems, loc_sems,
):
    rep, seq = lax.axis_index("rep"), lax.axis_index("seq")
    z, yh = lax.div(rep, jnp.int32(2)), mod(rep, 2)
    x, yl, c = lax.div(seq, jnp.int32(4)), mod(lax.div(seq, jnp.int32(2)), 2), mod(seq, 2)
    y = yh * 2 + yl
    oc, oyh = 1 - c, 1 - yh

    def dev(x_, y_, z_, c_):
        return {"rep": z_ * 2 + lax.div(y_, jnp.int32(2)), "seq": x_ * 4 + mod(y_, 2) * 2 + c_}

    def xd(k):
        return dev(mod(x + k, 4), y, z, c)

    def yd(k):
        return dev(x, mod(y + k, 4), z, c)

    def zd(k):
        return dev(x, y, mod(z + k, 8), c)

    partner = dev(x, y, z, oc)
    across = dev(x, 3 - y, z, c)
    group = [(dx, dl) for dx in range(4) for dl in range(2) if dx or dl]

    def gd(dx, dl):
        return dev(mod(x + dx, 4), yh * 2 + mod(yl + dl, 2), z, c)

    def place(dx, dl):
        return mod(x + dx, 4) * 2 + mod(yl + dl, 2)

    here = x * 2 + yl
    xm, xp = mod(x + 3, 4), mod(x + 1, 4)
    ym, yp = mod(y + 3, 4), mod(y + 1, 4)
    ymh, yml, yph, ypl = lax.div(ym, jnp.int32(2)), mod(ym, 2), lax.div(yp, jnp.int32(2)), mod(yp, 2)
    lane_c = pl.ds(pl.multiple_of(c * HD, HD), HD)
    lane_o = pl.ds(pl.multiple_of(oc * HD, HD), HD)
    mine = pl.ds(pl.multiple_of(c * 512, 512), 512)

    def cols(p):
        return pl.ds(pl.multiple_of(mod(z + OFF[p], 8) * 512, 512), 512)

    plane = [(dx, dy) for dx in (2, 1, 3, 0) for dy in (2, 1, 3, 0) if dx or dy]
    peers = [partner] + [dev(x, y, mod(z + k, 8), c_) for k in (4, 3, 5, 2, 6, 1, 7) for c_ in (c, oc)]
    peers += [dev(mod(x + dx, 4), mod(y + dy, 4), z, c_) for dx, dy in plane for c_ in (c, oc)]
    bar = pltpu.get_barrier_semaphore()
    for to in peers:
        pl.semaphore_signal(bar, inc=1, device_id=to, device_id_type=MESH)
    loads = [
        pltpu.make_async_copy(src, dst, loc_sems.at[i])
        for i, (src, dst) in enumerate(
            (
                (wk.at[x, yl, :, lane_c], w1.at[0, yh, x, yl]),
                (wv.at[x, yl, :, lane_c], w2.at[0, yh, x, yl]),
                (wq.at[:, :, :, lane_c], w0.at[0, yh]),
                (tok_hbm, tok.at[mine]),
                (cot.at[:, lane_c], cotb.at[c]),
            )
        )
    ]
    for cp in loads:
        cp.start()
    for cp in loads[:3]:
        cp.wait()
    pl.semaphore_wait(bar, len(peers))

    net = Net(send_sems, recv_sems, sizes, partner)

    ga, gb, gc, ge = GROUPS
    steps = {g: Batch(net) for g in GROUPS[1:]}
    for k in (1, 7, 2, 6, 3, 5, 4):
        to = SLOT[back(k)]
        for g in GROUPS[1:]:
            if to in range(*g):
                for w in (w1, w2):
                    steps[g].send(w.at[0, yh, x, yl], w.at[to, yh, x, yl], zd(k))

    def slots(g):
        return pl.ds(g[0], g[1] - g[0])

    def mid(g):
        if g in steps:
            steps[g].wait()
        b, c_ = w1.at[slots(g), yh, x, yl], w2.at[slots(g), yh, x, yl]
        return net.some([t for k in (1, 3, 2) for t in ((b, b, yd(k)), (c_, c_, xd(k)))])

    def wide(g, prev):
        prev.wait()
        b = [w1.at[slots(g), h, x] for h in (0, 1)]
        c_ = [w2.at[slots(g), yh, pl.ds(2 * h, 2), yl] for h in (0, 1)]
        lead = net.some([t for h, k in ((0, 1), (1, 3)) for t in ((b[h], b[h], xd(k)), (c_[h], c_[h], yd(k)))])
        rest = net.some([t for h, k in ((1, 1), (0, 3)) for t in ((b[h], b[h], xd(k)), (c_[h], c_[h], yd(k)))])
        return lead, rest

    def pass_on(g, prev):
        lead, rest = prev
        lead.wait()
        for ref, to in (
            (w1.at[slots(g), 0, xm], xd(1)),
            (w1.at[slots(g), 1, xp], xd(3)),
            (w2.at[slots(g), ymh, pl.ds(0, 2), yml], yd(1)),
            (w2.at[slots(g), yph, pl.ds(2, 2), ypl], yd(3)),
        ):
            rest.send(ref, ref, to)
        return rest

    def a_send(k, *parts):
        sends = []
        for half, way in parts:
            at, to = (back(k), back(k + 1)) if way == 0 else (k, k + 1)
            sends.append((w0.at[SLOT[at], half], w0.at[SLOT[to], half], zd(1 if way == 0 else 7)))
        return net.some(sends)

    def a_half(prev, half, k):
        prev.wait()
        return a_send(k, (half, 0), (half, 1))

    m_a = mid(ga)
    a_y = net.one(w0.at[0, yh], w0.at[0, yh], across)
    a1 = [a_send(0, (yh, 0), (yh, 1))]
    cot_x = net.one(cot.at[:, lane_o], cotb.at[c], partner)
    tok_x = net.one(tok_hbm, tok.at[mine], partner)

    def project(ps, lanes, ws, first):
        @pl.loop(0, 2)
        def _(i):
            r = pl.ds(pl.multiple_of(i * 512, 512), 512)
            got = None
            for p in ps:
                w = jnp.concatenate([w[p].reshape(512, HD) for w in ws], 1)
                term = dot(tok[r, cols(p)], w)
                got = term if got is None else got + term
            acc[r, lanes] = got if first else acc[r, lanes] + got

    def q_acc(*ps):
        project(ps, slice(0, 128), (w0,), ps[0] == 0)

    def kv_acc(g):
        project(range(*g), slice(128, 384), (w1, w2), g[0] == 0)

    m_b = mid(gb)
    n_a = wide(ga, m_a)
    a_y.wait()
    a1.append(a_send(0, (oyh, 0), (oyh, 1)))
    m_c = mid(gc)
    m_e = mid(ge)
    n_b = wide(gb, m_b)
    a2 = [a_half(a1[0], yh, 1)]
    f_a = pass_on(ga, n_a)
    n_c = wide(gc, m_c)
    a2.append(a_half(a1[1], oyh, 1))
    n_e = wide(ge, m_e)
    f_b = pass_on(gb, n_b)
    loads[3].wait()
    tok_x.wait()
    f_a.wait()
    kv_acc(ga)
    f_c = pass_on(gc, n_c)
    a3 = [a_half(a2[0], yh, 2)]
    q_acc(0)
    q_acc(1, 2)
    f_e = pass_on(ge, n_e)
    a3.append(a_half(a2[1], oyh, 2))
    f_b.wait()
    kv_acc(gb)
    f_c.wait()
    kv_acc(gc)
    for cp in a3:
        cp.wait()
    a4 = a_send(3, (0, 0), (1, 1))
    f_e.wait()
    w_x = [net.one(w1, o1, partner), net.one(w2, o2, partner)]
    kv_acc(ge)

    rows = [slice(0, 512), slice(512, 1024)]
    state = []
    for r in rows:
        qkv[r, 128:384] = acc[r, 128:384].astype(bf16)
        state.append(dot(qkv[r, 128:256], qkv[r, 256:384], 0, 0))
    st_snd[...] = (state[0] + state[1]).astype(bf16)
    prior[0] = jnp.zeros((HD, HD), f32)
    prior[1] = state[0]
    pair = net.n
    net.n += len(group)
    st = [
        net.send_if(place(dx, dl) > here, st_snd, st_rcv.at[i], gd(dx, dl), pair + i) for i, (dx, dl) in enumerate(group)
    ]

    q_acc(3, 4, 5, 6)
    a4.wait()
    w_x.append(net.one(w0, o0, partner))
    q_acc(7)
    qkv[:, 0:128] = acc[:, 0:128].astype(bf16)
    causal = lax.broadcasted_iota(jnp.int32, (512, 512), 0) >= lax.broadcasted_iota(jnp.int32, (512, 512), 1)
    for b, r in enumerate(rows):
        scores[b] = jnp.where(causal, dot(qkv[r, 0:128], qkv[r, 128:256], 1, 1), 0.0).astype(bf16)
        mixl[b] = dot(scores[b], qkv[r, 256:384])
    loads[4].wait()
    cot_x.wait()
    for i, (dx, dl) in enumerate(group):

        @pl.when(place(4 - dx, dl) < here)
        def _(i=i):
            st[i].wait_recv()
            got = st_rcv[i].astype(f32)
            prior[0] += got
            prior[1] += got

    back_state = []
    for b, r in enumerate(rows):
        p_hi, p_lo = split(prior[b])
        q = qkv[r, 0:128]
        mix = mixl[b] + (dot(q, p_hi) + dot(q, p_lo))
        s = lax.rsqrt(jnp.mean(mix * mix, -1, keepdims=True) + EPS)
        att_snd[b] = (mix * s).astype(bf16)
        g = cotb[b].astype(f32)
        m = jnp.mean(g * mix, -1, keepdims=True)
        dmix[b] = (s * g - s * s * s * mix * m).astype(bf16)
        back_state.append(dot(q, dmix[b], 0, 0))
    bk_snd[...] = (back_state[0] + back_state[1]).astype(bf16)
    later[1] = jnp.zeros((HD, HD), f32)
    later[0] = back_state[1]
    bk = [
        net.send_if(place(dx, dl) < here, bk_snd, bk_rcv.at[i], gd(dx, dl), pair + i) for i, (dx, dl) in enumerate(group)
    ]
    att_x = net.one(att_snd.at[oc], att_oth, partner)

    for b, r in enumerate(rows):
        q, k, v = qkv[r, 0:128], qkv[r, 128:256], qkv[r, 256:384]
        bs = jnp.where(causal, dot(dmix[b], v, 1, 1), 0.0).astype(bf16)
        p_hi, p_lo = split(prior[b])
        d_all[r, 0:128] = (dot(bs, k) + (dot(dmix[b], p_hi, 1, 1) + dot(dmix[b], p_lo, 1, 1))).astype(bf16)
        mixl[b] = dot(bs, q, 0, 0)
        d_loc[b] = dot(scores[b], dmix[b], 0, 0)

    def p_q(p):
        p0[p] = dot(tok[:, cols(p)], d_all[:, 0:128], 0, 0).reshape(BLK[1:])

    def p_kv(g):
        for p in range(*g):
            got = dot(tok[:, cols(p)], d_all[:, 128:384], 0, 0)
            p1[p] = got[:, 0:128].reshape(BLK[1:])
            p2[p] = got[:, 128:256].reshape(BLK[1:])

    def p_qkv(g):
        for p in range(*g):
            got = dot(tok[:, cols(p)], d_all[...], 0, 0)
            p0[p] = got[:, 0:128].reshape(BLK[1:])
            p1[p] = got[:, 128:256].reshape(BLK[1:])
            p2[p] = got[:, 256:384].reshape(BLK[1:])

    def a_out(step, parts, plus=None):
        if plus is not None:
            plus.wait()
        sends = []
        for way, half in parts:
            k = 5 - step
            val = p0[SLOT[k if way == 0 else 8 - k], half]
            if plus is not None:
                val = val + ra[way, step - 2, half].astype(f32)
            sa[way, step - 1, half] = val.astype(bf16)
            sends.append((sa.at[way, step - 1, half], ra.at[way, step - 1, half], zd(1 if way == 0 else 7)))
        return net.some(sends)

    ends, free = ((0, 0), (1, 1)), ((0, 1), (1, 0))
    p_q(7)
    r1 = a_out(1, ends)
    p_q(5)
    p_q(6)
    r2f = a_out(2, free)

    for i, (dx, dl) in enumerate(group):

        @pl.when(place(4 - dx, dl) > here)
        def _(i=i):
            bk[i].wait_recv()
            got = bk_rcv[i].astype(f32)
            later[0] += got
            later[1] += got

    r2 = a_out(2, ends, r1)
    for b, r in enumerate(rows):
        l_hi, l_lo = split(later[b])
        k, v = qkv[r, 128:256], qkv[r, 256:384]
        d_all[r, 128:256] = (mixl[b] + (dot(v, l_hi, 1, 1) + dot(v, l_lo, 1, 1))).astype(bf16)
        d_all[r, 256:384] = (d_loc[b] + (dot(k, l_hi) + dot(k, l_lo))).astype(bf16)
    d_x = net.one(d_all.at[pl.ds(pl.multiple_of(oc * 512, 512), 512)], d_oth, partner)

    def direct(g):
        out = Batch(net)
        for k in (2, 1, 3):
            sb_d[k - 1, slots(g)] = p1[slots(g), :, mod(x + k, 4)].astype(bf16)
            out.send(sb_d.at[k - 1, slots(g)], rb_d.at[k - 1, slots(g)], xd(k))
            at = mod(y + k, 4)
            sc_d[k - 1, slots(g)] = p2[slots(g), lax.div(at, jnp.int32(2)), :, mod(at, 2)].astype(bf16)
            out.send(sc_d.at[k - 1, slots(g)], rc_d.at[k - 1, slots(g)], yd(k))
        return out

    def third(g, prev):
        prev.wait()
        acc_b[slots(g)] = p1[slots(g), :, x] + sum(rb_d[k, slots(g)].astype(f32) for k in range(3))
        acc_c[slots(g)] = p2[slots(g), yh, :, yl] + sum(rc_d[k, slots(g)].astype(f32) for k in range(3))
        out = Batch(net)
        for k in (2, 1, 3):
            at = mod(y + k, 4)
            sb_y[k - 1, slots(g)] = acc_b[slots(g), lax.div(at, jnp.int32(2)), mod(at, 2)].astype(bf16)
            out.send(sb_y.at[k - 1, slots(g)], rb_y.at[k - 1, slots(g)], yd(k))
            sc_x[k - 1, slots(g)] = acc_c[slots(g), mod(x + k, 4)].astype(bf16)
            out.send(sc_x.at[k - 1, slots(g)], rc_x.at[k - 1, slots(g)], xd(k))
        return out

    last = Batch(net)

    def fourth(g, prev):
        prev.wait()
        n = g[1] - g[0]
        got = acc_b[slots(g), yh, yl] + sum(rb_y[k, slots(g)].astype(f32) for k in range(3))
        acc_b2[slots(g)] = got.reshape(n, 2, 16, HD)
        got = acc_c[slots(g), x] + sum(rc_x[k, slots(g)].astype(f32) for k in range(3))
        acc_c2[slots(g)] = got.reshape(n, 2, 16, HD)
        for snd, rcv, total in ((sb_z, rb_z, acc_b2), (sc_z, rc_z, acc_c2)):
            snd[slots(g)] = total[slots(g)].astype(bf16)
            for p in range(*g):
                k = OFF[p]
                to = SLOT[back(k)]
                if k:
                    last.send(snd.at[p, c], rcv.at[0, to], zd(k))
                last.send(snd.at[p, oc], rcv.at[1, to], dev(x, y, mod(z + k, 8), oc) if k else partner)

    def g_t(*ps):
        for p in ps:
            w = jnp.concatenate([ref[p].reshape(512, HD) for ref in (w0, w1, w2, o0, o1, o2)], 1)
            d = jnp.concatenate([d_all[mine, :], d_oth[...]], 1)
            gt_o[:, cols(p)] = dot(d, w, 1, 1).astype(bf16)

    p_kv(ge)
    d_e = direct(ge)
    p_qkv(gc)
    d_c = direct(gc)
    r3f = a_out(3, free, r2f)
    p_qkv(gb)
    d_b = direct(gb)
    r3 = a_out(3, ends, r2)
    p_qkv(ga)
    d_a = direct(ga)
    d_x.wait()
    for cp in w_x:
        cp.wait()
    g_t(0)
    r4f = a_out(4, free, r3f)
    r4 = a_out(4, ends, r3)
    g_t(1, 2)
    t_e = third(ge, d_e)
    t_c = third(gc, d_c)
    g_t(3)
    t_b = third(gb, d_b)
    t_a = third(ga, d_a)
    r4f.wait()
    r4.wait()
    acc_a[...] = (p0[0] + ra[0, 3].astype(f32) + ra[1, 3].astype(f32)).reshape(2, 4, 2, 2, 16, HD)
    sa_x[...] = acc_a[...].astype(bf16)
    for i, (dx, dy) in enumerate(plane):
        ax, ay = mod(x + dx, 4), mod(y + dy, 4)
        part = sa_x.at[lax.div(ay, jnp.int32(2)), ax, mod(ay, 2)]
        last.send(part.at[c], ra_x.at[0, i], dev(ax, ay, z, c))
        last.send(part.at[oc], ra_x.at[1, i], dev(ax, ay, z, oc))
    last.send(sa_x.at[yh, x, yl, oc], ra_x.at[1, 15], partner)
    fourth(ge, t_e)
    fourth(gc, t_c)
    g_t(4)
    fourth(gb, t_b)
    g_t(5)
    fourth(ga, t_a)
    g_t(6, 7)
    att_o[:, lane_c] = att_snd[c]
    att_x.wait()
    att_o[:, lane_o] = att_oth[...]
    scale = 1.0 / T_DEV
    last.wait()
    gq_o[:, lane_c] = (acc_a[yh, x, yl, c] + sum(ra_x[0, k].astype(f32) for k in range(15))) * scale
    gq_o[:, lane_o] = sum(ra_x[1, k].astype(f32) for k in range(16)) * scale
    for out, total, rcv in ((gk_o, acc_b2, rb_z), (gv_o, acc_c2, rc_z)):
        out[:, lane_c] = (total[0, c] + sum(rcv[0, p].astype(f32) for p in range(1, 8))) * scale
        out[:, lane_o] = sum(rcv[1, p].astype(f32) for p in range(8)) * scale
    net.finish()


def write_out(*refs):
    sems = refs[10]
    copies = [pltpu.make_async_copy(refs[i], refs[5 + i], sems.at[i]) for i in (1, 0, 2, 3, 4)]
    for cp in copies:
        cp.start()
    for cp in copies:
        cp.wait()


def body(tokens, w_query, w_key, w_value, cotangent):
    vm, any_ = pl.BlockSpec(memory_space=pltpu.VMEM), pl.BlockSpec(memory_space=pl.ANY)
    hbm = pl.BlockSpec(memory_space=pltpu.HBM)

    def v(*shape, t=bf16):
        return pltpu.VMEM(shape, t)

    scratch = [v(1024, D)] + [v(*BLK)] * 6
    scratch += [v(1024, 384, t=f32), v(1024, 384), v(2, 512, 128), v(2, 512, 512), v(2, 512, 128, t=f32), v(2, 512, 128, t=f32), v(2, 512, 128)]
    scratch += [v(1024, 384), v(512, 384), v(512, 128), v(2, 512, 128)]
    scratch += [v(128, 128), v(7, 128, 128), v(128, 128), v(7, 128, 128), v(2, 128, 128, t=f32), v(2, 128, 128, t=f32)]
    scratch += [v(*BLK, t=f32)] * 3
    scratch += [v(2, 4, 2, 4, 2, 32, 128)] * 2
    scratch += [v(2, 4, 2, 2, 16, 128, t=f32), v(8, 2, 2, 32, 128, t=f32), v(8, 4, 32, 128, t=f32)]
    scratch += [v(2, 4, 2, 2, 16, 128), v(2, 16, 16, 128)]
    scratch += [v(3, 8, 32, 128)] * 2 + [v(8, 2, 16, 128), v(2, 8, 16, 128)] + [v(8, 2, 16, 128, t=f32)]
    scratch += [v(3, 8, 32, 128)] * 2 + [v(8, 2, 16, 128), v(2, 8, 16, 128)] + [v(8, 2, 16, 128, t=f32)]
    scratch += [v(3, 8, 2, 2, 32, 128)] * 2 + [v(3, 8, 4, 32, 128)] * 2 + [v(160, 16, 128)]
    scratch += [pltpu.SemaphoreType.DMA((N_SEM,)), pltpu.SemaphoreType.DMA((N_SEM,)), pltpu.SemaphoreType.DMA((5,))]
    grad = pltpu.VMEM((16, 256), f32)
    args = [tokens] + [w.reshape(4, 2, 32, 256) for w in (w_query, w_key, w_value)] + [cotangent]
    outs = pl.pallas_call(
        kernel,
        out_shape=(
            pltpu.VMEM((T_DEV, 256), bf16),
            pltpu.VMEM((T_DEV, D), bf16),
            grad,
            grad,
            grad,
        ),
        in_specs=[hbm] * 5,
        out_specs=(vm, vm, vm, vm, vm),
        scratch_shapes=scratch,
        compiler_params=pltpu.CompilerParams(collective_id=0, has_side_effects=True, vmem_limit_bytes=48 * 2**20),
        cost_estimate=pl.CostEstimate(flops=10**10, bytes_accessed=10**7, transcendentals=1024),
        name="step",
    )(*[pltpu.with_memory_space_constraint(a, pltpu.HBM) for a in args])
    return pl.pallas_call(
        write_out,
        out_shape=[jax.ShapeDtypeStruct(o.shape, o.dtype) for o in outs],
        in_specs=[vm] * 5,
        out_specs=[any_] * 5,
        scratch_shapes=[pltpu.SemaphoreType.DMA((5,))],
        compiler_params=pltpu.CompilerParams(vmem_limit_bytes=2**20),
        name="write_out",
    )(*[pltpu.with_memory_space_constraint(o, pltpu.VMEM) for o in outs])


def solution(mesh):
    both = P(("rep", "seq"), None)
    rep = P("rep", None)
    return jax.shard_map(
        body, mesh=mesh, in_specs=(both, rep, rep, rep, both), out_specs=(both,) * 5, check_vma=False
    )
```

```python
import math

import jax
import jax.numpy as jnp
from jax import lax
from jax.experimental import pallas as pl
from jax.experimental.pallas import tpu as pltpu
from jax.sharding import PartitionSpec as P

D = 4096
HD = 128
T_DEV = 512
EPS = 1e-06
MESH = pl.DeviceIdType.MESH
f32 = jnp.float32
bf16 = jnp.bfloat16
N_SEM = 53
BLK = (8, 2, 4, 2, 32, 128)


def mod(a, n):
    return lax.rem(a, jnp.int32(n))


def dot(a, b, ca=1, cb=0):
    return lax.dot_general(a, b, (((ca,), (cb,)), ((), ())), preferred_element_type=f32)


def split(a):
    hi = a.astype(bf16)
    return hi, (a - hi.astype(f32)).astype(bf16)


class Batch:
    def __init__(self, net):
        self.net, self.i, self.copies, self.units = net, net.n, [], 0
        net.n += 1
        assert net.n <= N_SEM
        net.batches.append(self)

    def send(self, src, dst, to):
        cp = self.net.make(src, dst, to, self.i)
        cp.start()
        self.copies.append(cp)
        self.units += math.prod(src.shape) // 2048

    def all(self):
        if len(self.copies) == 1:
            return self.copies[0]
        ref = self.net.sizes.at[pl.ds(0, self.units)]
        return self.net.make(ref, ref, self.net.anyone, self.i)

    def wait(self):
        self.all().wait_recv()


class Net:
    def __init__(self, send_sems, recv_sems, sizes, anyone):
        self.ss, self.rs, self.sizes, self.anyone = send_sems, recv_sems, sizes, anyone
        self.n, self.batches, self.maybe = 0, [], []

    def make(self, src, dst, to, i):
        return pltpu.make_async_remote_copy(
            src_ref=src, dst_ref=dst, send_sem=self.ss.at[i], recv_sem=self.rs.at[i], device_id=to, device_id_type=MESH
        )

    def one(self, src, dst, to):
        b = Batch(self)
        b.send(src, dst, to)
        return b

    def some(self, sends):
        b = Batch(self)
        for src, dst, to in sends:
            b.send(src, dst, to)
        return b

    def send_if(self, cond, src, dst, to, i):
        cp = self.make(src, dst, to, i)
        pl.when(cond)(cp.start)
        self.maybe.append((cp, cond))
        return cp

    def finish(self):
        for b in self.batches:
            b.all().wait_send()
        for cp, cond in self.maybe:
            pl.when(cond)(cp.wait_send)


OFF = (0, 1, 7, 2, 6, 3, 5, 4)
SLOT = {k: p for p, k in enumerate(OFF)}
GROUPS = ((0, 1), (1, 3), (3, 5), (5, 8))


def back(k):
    return (8 - k) % 8


def kernel(
    tok_hbm, wq, wk, wv, cot, att_o, gt_o, gq_o, gk_o, gv_o,
    tok, w0, w1, w2, o0, o1, o2, acc, qkv, cotb, scores, mixl, d_loc, dmix, d_all, d_oth, att_oth, att_snd,
    st_snd, st_rcv, bk_snd, bk_rcv, prior, later,
    p0, p1, p2, sa, ra, acc_a, acc_b, acc_c,
    sa_x, ra_x, sb_y, rb_y, sb_z, rb_z, acc_b2, sc_x, rc_x, sc_z, rc_z, acc_c2,
    sb_d, rb_d, sc_d, rc_d, sizes, send_sems, recv_sems, loc_sems,
):
    rep, seq = lax.axis_index("rep"), lax.axis_index("seq")
    z, yh = lax.div(rep, jnp.int32(2)), mod(rep, 2)
    x, yl, c = lax.div(seq, jnp.int32(4)), mod(lax.div(seq, jnp.int32(2)), 2), mod(seq, 2)
    y = yh * 2 + yl
    oc, oyh = 1 - c, 1 - yh

    def dev(x_, y_, z_, c_):
        return {"rep": z_ * 2 + lax.div(y_, jnp.int32(2)), "seq": x_ * 4 + mod(y_, 2) * 2 + c_}

    def xd(k):
        return dev(mod(x + k, 4), y, z, c)

    def yd(k):
        return dev(x, mod(y + k, 4), z, c)

    def zd(k):
        return dev(x, y, mod(z + k, 8), c)

    partner = dev(x, y, z, oc)
    across = dev(x, 3 - y, z, c)
    group = [(dx, dl) for dx in (2, 1, 3, 0) for dl in (1, 0) if dx or dl]

    def gd(dx, dl):
        return dev(mod(x + dx, 4), yh * 2 + mod(yl + dl, 2), z, c)

    def place(dx, dl):
        return mod(x + dx, 4) * 2 + mod(yl + dl, 2)

    here = x * 2 + yl
    xm, xp = mod(x + 3, 4), mod(x + 1, 4)
    ym, yp = mod(y + 3, 4), mod(y + 1, 4)
    ymh, yml, yph, ypl = lax.div(ym, jnp.int32(2)), mod(ym, 2), lax.div(yp, jnp.int32(2)), mod(yp, 2)
    lane_c = pl.ds(pl.multiple_of(c * HD, HD), HD)
    lane_o = pl.ds(pl.multiple_of(oc * HD, HD), HD)
    mine = pl.ds(pl.multiple_of(c * 512, 512), 512)

    def cols(p):
        return pl.ds(pl.multiple_of(mod(z + OFF[p], 8) * 512, 512), 512)

    plane = [(dx, dy) for dx in (2, 1, 3, 0) for dy in (2, 1, 3, 0) if dx or dy]
    peers = [partner] + [dev(x, y, mod(z + k, 8), c_) for k in (4, 3, 5, 2, 6, 1, 7) for c_ in (c, oc)]
    peers += [dev(mod(x + dx, 4), mod(y + dy, 4), z, c_) for dx, dy in plane for c_ in (c, oc)]
    bar = pltpu.get_barrier_semaphore()
    for to in peers:
        pl.semaphore_signal(bar, inc=1, device_id=to, device_id_type=MESH)
    loads = [
        pltpu.make_async_copy(src, dst, loc_sems.at[i])
        for i, (src, dst) in enumerate(
            (
                (wk.at[x, yl, :, lane_c], w1.at[0, yh, x, yl]),
                (wv.at[x, yl, :, lane_c], w2.at[0, yh, x, yl]),
                (wq.at[:, :, :, lane_c], w0.at[0, yh]),
                (tok_hbm, tok.at[mine]),
                (cot.at[:, lane_c], cotb.at[c]),
            )
        )
    ]
    for cp in loads:
        cp.start()
    for cp in loads[:3]:
        cp.wait()
    pl.semaphore_wait(bar, len(peers))

    net = Net(send_sems, recv_sems, sizes, partner)

    ga, gb, gc, ge = GROUPS
    steps = {g: Batch(net) for g in GROUPS[1:]}
    for k in (1, 7, 2, 6, 3, 5, 4):
        to = SLOT[back(k)]
        for g in GROUPS[1:]:
            if to in range(*g):
                for w in (w1, w2):
                    steps[g].send(w.at[0, yh, x, yl], w.at[to, yh, x, yl], zd(k))

    def slots(g):
        return pl.ds(g[0], g[1] - g[0])

    def mid(g):
        if g in steps:
            steps[g].wait()
        b, c_ = w1.at[slots(g), yh, x, yl], w2.at[slots(g), yh, x, yl]
        return net.some([t for k in (1, 3, 2) for t in ((b, b, yd(k)), (c_, c_, xd(k)))])

    def wide(g, prev):
        prev.wait()
        b = [w1.at[slots(g), h, x] for h in (0, 1)]
        c_ = [w2.at[slots(g), yh, pl.ds(2 * h, 2), yl] for h in (0, 1)]
        lead = net.some([t for h, k in ((0, 1), (1, 3)) for t in ((b[h], b[h], xd(k)), (c_[h], c_[h], yd(k)))])
        rest = net.some([t for h, k in ((1, 1), (0, 3)) for t in ((b[h], b[h], xd(k)), (c_[h], c_[h], yd(k)))])
        return lead, rest

    def pass_on(g, prev):
        lead, rest = prev
        lead.wait()
        for ref, to in (
            (w1.at[slots(g), 0, xm], xd(1)),
            (w1.at[slots(g), 1, xp], xd(3)),
            (w2.at[slots(g), ymh, pl.ds(0, 2), yml], yd(1)),
            (w2.at[slots(g), yph, pl.ds(2, 2), ypl], yd(3)),
        ):
            rest.send(ref, ref, to)
        return rest

    def a_send(k, *parts):
        sends = []
        for half, way in parts:
            at, to = (back(k), back(k + 1)) if way == 0 else (k, k + 1)
            sends.append((w0.at[SLOT[at], half], w0.at[SLOT[to], half], zd(1 if way == 0 else 7)))
        return net.some(sends)

    def a_half(prev, half, k):
        prev.wait()
        return a_send(k, (half, 0), (half, 1))

    m_a = mid(ga)
    a_y = net.one(w0.at[0, yh], w0.at[0, yh], across)
    a1 = [a_send(0, (yh, 0), (yh, 1))]
    cot_x = net.one(cot.at[:, lane_o], cotb.at[c], partner)
    tok_x = net.one(tok_hbm, tok.at[mine], partner)

    rows = [slice(0, 512), slice(512, 1024)]

    def project(ps, lanes, ws, first):
        for r in rows:
            got = None
            for p in ps:
                w = jnp.concatenate([w[p].reshape(512, HD) for w in ws], 1)
                term = dot(tok[r, cols(p)], w)
                got = term if got is None else got + term
            acc[r, lanes] = got if first else acc[r, lanes] + got

    def q_acc(*ps):
        project(ps, slice(0, 128), (w0,), ps[0] == 0)

    def kv_acc(g):
        project(range(*g), slice(128, 384), (w1, w2), g[0] == 0)

    m_b = mid(gb)
    n_a = wide(ga, m_a)
    a_y.wait()
    a1.append(a_send(0, (oyh, 0), (oyh, 1)))
    m_c = mid(gc)
    m_e = mid(ge)
    n_b = wide(gb, m_b)
    a2 = [a_half(a1[0], yh, 1)]
    f_a = pass_on(ga, n_a)
    n_c = wide(gc, m_c)
    a2.append(a_half(a1[1], oyh, 1))
    n_e = wide(ge, m_e)
    f_b = pass_on(gb, n_b)
    loads[3].wait()
    tok_x.wait()
    f_a.wait()
    kv_acc(ga)
    f_c = pass_on(gc, n_c)
    a3 = [a_half(a2[0], yh, 2)]
    q_acc(0)
    q_acc(1, 2)
    f_e = pass_on(ge, n_e)
    a3.append(a_half(a2[1], oyh, 2))
    f_b.wait()
    kv_acc(gb)
    f_c.wait()
    kv_acc(gc)
    for cp in a3:
        cp.wait()
    a4 = a_send(3, (0, 0), (1, 1))
    f_e.wait()
    w_x = [net.one(w1, o1, partner), net.one(w2, o2, partner)]
    kv_acc(ge)

    state = []
    for r in rows:
        qkv[r, 128:384] = acc[r, 128:384].astype(bf16)
        state.append(dot(qkv[r, 128:256], qkv[r, 256:384], 0, 0))
    st_snd[...] = (state[0] + state[1]).astype(bf16)
    prior[0] = jnp.zeros((HD, HD), f32)
    prior[1] = state[0]
    pair = net.n
    net.n += len(group)
    st = [
        net.send_if(place(dx, dl) > here, st_snd, st_rcv.at[i], gd(dx, dl), pair + i) for i, (dx, dl) in enumerate(group)
    ]

    q_acc(3, 4, 5, 6)
    a4.wait()
    w_x.append(net.one(w0, o0, partner))
    q_acc(7)
    qkv[:, 0:128] = acc[:, 0:128].astype(bf16)
    causal = lax.broadcasted_iota(jnp.int32, (512, 512), 0) >= lax.broadcasted_iota(jnp.int32, (512, 512), 1)
    for b, r in enumerate(rows):
        scores[b] = jnp.where(causal, dot(qkv[r, 0:128], qkv[r, 128:256], 1, 1), 0.0).astype(bf16)
        mixl[b] = dot(scores[b], qkv[r, 256:384])
    loads[4].wait()
    cot_x.wait()
    for i, (dx, dl) in enumerate(group):

        @pl.when(place(4 - dx, dl) < here)
        def _(i=i):
            st[i].wait_recv()
            got = st_rcv[i].astype(f32)
            prior[0] += got
            prior[1] += got

    back_state = []
    for b, r in enumerate(rows):
        p_hi, p_lo = split(prior[b])
        q = qkv[r, 0:128]
        mix = mixl[b] + (dot(q, p_hi) + dot(q, p_lo))
        s = lax.rsqrt(jnp.mean(mix * mix, -1, keepdims=True) + EPS)
        att_snd[b] = (mix * s).astype(bf16)
        g = cotb[b].astype(f32)
        m = jnp.mean(g * mix, -1, keepdims=True)
        dmix[b] = (s * g - s * s * s * mix * m).astype(bf16)
        back_state.append(dot(q, dmix[b], 0, 0))
    bk_snd[...] = (back_state[0] + back_state[1]).astype(bf16)
    later[1] = jnp.zeros((HD, HD), f32)
    later[0] = back_state[1]
    bk = [
        net.send_if(place(dx, dl) < here, bk_snd, bk_rcv.at[i], gd(dx, dl), pair + i) for i, (dx, dl) in enumerate(group)
    ]
    att_x = net.one(att_snd.at[oc], att_oth, partner)

    for b, r in enumerate(rows):
        q, k, v = qkv[r, 0:128], qkv[r, 128:256], qkv[r, 256:384]
        bs = jnp.where(causal, dot(dmix[b], v, 1, 1), 0.0).astype(bf16)
        p_hi, p_lo = split(prior[b])
        d_all[r, 0:128] = (dot(bs, k) + (dot(dmix[b], p_hi, 1, 1) + dot(dmix[b], p_lo, 1, 1))).astype(bf16)
        mixl[b] = dot(bs, q, 0, 0)
        d_loc[b] = dot(scores[b], dmix[b], 0, 0)

    def p_q(p):
        p0[p] = dot(tok[:, cols(p)], d_all[:, 0:128], 0, 0).reshape(BLK[1:])

    def p_kv(g):
        for p in range(*g):
            got = dot(tok[:, cols(p)], d_all[:, 128:384], 0, 0)
            p1[p] = got[:, 0:128].reshape(BLK[1:])
            p2[p] = got[:, 128:256].reshape(BLK[1:])

    def p_qkv(g):
        for p in range(*g):
            got = dot(tok[:, cols(p)], d_all[...], 0, 0)
            p0[p] = got[:, 0:128].reshape(BLK[1:])
            p1[p] = got[:, 128:256].reshape(BLK[1:])
            p2[p] = got[:, 256:384].reshape(BLK[1:])

    def a_out(step, parts, plus=None):
        if plus is not None:
            plus.wait()
        sends = []
        for way, half in parts:
            k = 5 - step
            val = p0[SLOT[k if way == 0 else 8 - k], half]
            if plus is not None:
                val = val + ra[way, step - 2, half].astype(f32)
            sa[way, step - 1, half] = val.astype(bf16)
            sends.append((sa.at[way, step - 1, half], ra.at[way, step - 1, half], zd(1 if way == 0 else 7)))
        return net.some(sends)

    ends, free = ((0, 0), (1, 1)), ((0, 1), (1, 0))
    p_q(7)
    r1 = a_out(1, ends)
    p_q(5)
    p_q(6)
    r2f = a_out(2, free)
    p_q(3)
    p_q(4)

    for i, (dx, dl) in enumerate(group):

        @pl.when(place(4 - dx, dl) > here)
        def _(i=i):
            bk[i].wait_recv()
            got = bk_rcv[i].astype(f32)
            later[0] += got
            later[1] += got

    r2 = a_out(2, ends, r1)
    for b, r in enumerate(rows):
        l_hi, l_lo = split(later[b])
        k, v = qkv[r, 128:256], qkv[r, 256:384]
        d_all[r, 128:256] = (mixl[b] + (dot(v, l_hi, 1, 1) + dot(v, l_lo, 1, 1))).astype(bf16)
        d_all[r, 256:384] = (d_loc[b] + (dot(k, l_hi) + dot(k, l_lo))).astype(bf16)
    d_x = net.one(d_all.at[pl.ds(pl.multiple_of(oc * 512, 512), 512)], d_oth, partner)

    def direct(g):
        out = Batch(net)
        for k in (2, 1, 3):
            sb_d[k - 1, slots(g)] = p1[slots(g), :, mod(x + k, 4)].astype(bf16)
            out.send(sb_d.at[k - 1, slots(g)], rb_d.at[k - 1, slots(g)], xd(k))
            at = mod(y + k, 4)
            sc_d[k - 1, slots(g)] = p2[slots(g), lax.div(at, jnp.int32(2)), :, mod(at, 2)].astype(bf16)
            out.send(sc_d.at[k - 1, slots(g)], rc_d.at[k - 1, slots(g)], yd(k))
        return out

    def third(g, prev):
        prev.wait()
        acc_b[slots(g)] = p1[slots(g), :, x] + sum(rb_d[k, slots(g)].astype(f32) for k in range(3))
        acc_c[slots(g)] = p2[slots(g), yh, :, yl] + sum(rc_d[k, slots(g)].astype(f32) for k in range(3))
        out = Batch(net)
        for k in (2, 1, 3):
            at = mod(y + k, 4)
            sb_y[k - 1, slots(g)] = acc_b[slots(g), lax.div(at, jnp.int32(2)), mod(at, 2)].astype(bf16)
            out.send(sb_y.at[k - 1, slots(g)], rb_y.at[k - 1, slots(g)], yd(k))
            sc_x[k - 1, slots(g)] = acc_c[slots(g), mod(x + k, 4)].astype(bf16)
            out.send(sc_x.at[k - 1, slots(g)], rc_x.at[k - 1, slots(g)], xd(k))
        return out

    last = Batch(net)

    def fourth(g, prev):
        prev.wait()
        n = g[1] - g[0]
        got = acc_b[slots(g), yh, yl] + sum(rb_y[k, slots(g)].astype(f32) for k in range(3))
        acc_b2[slots(g)] = got.reshape(n, 2, 16, HD)
        got = acc_c[slots(g), x] + sum(rc_x[k, slots(g)].astype(f32) for k in range(3))
        acc_c2[slots(g)] = got.reshape(n, 2, 16, HD)
        for snd, rcv, total in ((sb_z, rb_z, acc_b2), (sc_z, rc_z, acc_c2)):
            snd[slots(g)] = total[slots(g)].astype(bf16)
            for p in range(*g):
                k = OFF[p]
                to = SLOT[back(k)]
                if k:
                    last.send(snd.at[p, c], rcv.at[0, to], zd(k))
                last.send(snd.at[p, oc], rcv.at[1, to], dev(x, y, mod(z + k, 8), oc) if k else partner)

    def g_t(*ps):
        for p in ps:
            w = jnp.concatenate([ref[p].reshape(512, HD) for ref in (w0, w1, w2, o0, o1, o2)], 1)
            d = jnp.concatenate([d_all[mine, :], d_oth[...]], 1)
            gt_o[:, cols(p)] = dot(d, w, 1, 1).astype(bf16)

    p_kv(ge)
    d_e = direct(ge)
    p_kv(gc)
    d_c = direct(gc)
    r3f = a_out(3, free, r2f)
    p_qkv(gb)
    d_b = direct(gb)
    r3 = a_out(3, ends, r2)
    p_qkv(ga)
    d_a = direct(ga)
    d_x.wait()
    for cp in w_x:
        cp.wait()
    g_t(0)
    r4f = a_out(4, free, r3f)
    r4 = a_out(4, ends, r3)
    g_t(1, 2)
    t_e = third(ge, d_e)
    t_c = third(gc, d_c)
    g_t(3)
    t_b = third(gb, d_b)
    t_a = third(ga, d_a)
    r4f.wait()
    r4.wait()
    acc_a[...] = (p0[0] + ra[0, 3].astype(f32) + ra[1, 3].astype(f32)).reshape(2, 4, 2, 2, 16, HD)
    sa_x[...] = acc_a[...].astype(bf16)
    for i, (dx, dy) in enumerate(plane):
        ax, ay = mod(x + dx, 4), mod(y + dy, 4)
        part = sa_x.at[lax.div(ay, jnp.int32(2)), ax, mod(ay, 2)]
        last.send(part.at[c], ra_x.at[0, i], dev(ax, ay, z, c))
        last.send(part.at[oc], ra_x.at[1, i], dev(ax, ay, z, oc))
    last.send(sa_x.at[yh, x, yl, oc], ra_x.at[1, 15], partner)
    fourth(ge, t_e)
    fourth(gc, t_c)
    g_t(4)
    fourth(gb, t_b)
    g_t(5)
    fourth(ga, t_a)
    g_t(6, 7)
    att_o[:, lane_c] = att_snd[c]
    att_x.wait()
    att_o[:, lane_o] = att_oth[...]
    scale = 1.0 / T_DEV
    last.wait()
    gq_o[:, lane_c] = (acc_a[yh, x, yl, c] + sum(ra_x[0, k].astype(f32) for k in range(15))) * scale
    gq_o[:, lane_o] = sum(ra_x[1, k].astype(f32) for k in range(16)) * scale
    for out, total, rcv in ((gk_o, acc_b2, rb_z), (gv_o, acc_c2, rc_z)):
        out[:, lane_c] = (total[0, c] + sum(rcv[0, p].astype(f32) for p in range(1, 8))) * scale
        out[:, lane_o] = sum(rcv[1, p].astype(f32) for p in range(8)) * scale
    net.finish()


def write_out(*refs):
    sems = refs[10]
    copies = [pltpu.make_async_copy(refs[i], refs[5 + i], sems.at[i]) for i in (1, 0, 2, 3, 4)]
    for cp in copies:
        cp.start()
    for cp in copies:
        cp.wait()


def body(tokens, w_query, w_key, w_value, cotangent):
    vm, any_ = pl.BlockSpec(memory_space=pltpu.VMEM), pl.BlockSpec(memory_space=pl.ANY)
    hbm = pl.BlockSpec(memory_space=pltpu.HBM)

    def v(*shape, t=bf16):
        return pltpu.VMEM(shape, t)

    scratch = [v(1024, D)] + [v(*BLK)] * 6
    scratch += [v(1024, 384, t=f32), v(1024, 384), v(2, 512, 128), v(2, 512, 512), v(2, 512, 128, t=f32), v(2, 512, 128, t=f32), v(2, 512, 128)]
    scratch += [v(1024, 384), v(512, 384), v(512, 128), v(2, 512, 128)]
    scratch += [v(128, 128), v(7, 128, 128), v(128, 128), v(7, 128, 128), v(2, 128, 128, t=f32), v(2, 128, 128, t=f32)]
    scratch += [v(*BLK, t=f32)] * 3
    scratch += [v(2, 4, 2, 4, 2, 32, 128)] * 2
    scratch += [v(2, 4, 2, 2, 16, 128, t=f32), v(8, 2, 2, 32, 128, t=f32), v(8, 4, 32, 128, t=f32)]
    scratch += [v(2, 4, 2, 2, 16, 128), v(2, 16, 16, 128)]
    scratch += [v(3, 8, 32, 128)] * 2 + [v(8, 2, 16, 128), v(2, 8, 16, 128)] + [v(8, 2, 16, 128, t=f32)]
    scratch += [v(3, 8, 32, 128)] * 2 + [v(8, 2, 16, 128), v(2, 8, 16, 128)] + [v(8, 2, 16, 128, t=f32)]
    scratch += [v(3, 8, 2, 2, 32, 128)] * 2 + [v(3, 8, 4, 32, 128)] * 2 + [v(160, 16, 128)]
    scratch += [pltpu.SemaphoreType.DMA((N_SEM,)), pltpu.SemaphoreType.DMA((N_SEM,)), pltpu.SemaphoreType.DMA((5,))]
    grad = pltpu.VMEM((16, 256), f32)
    args = [tokens] + [w.reshape(4, 2, 32, 256) for w in (w_query, w_key, w_value)] + [cotangent]
    outs = pl.pallas_call(
        kernel,
        out_shape=(
            pltpu.VMEM((T_DEV, 256), bf16),
            pltpu.VMEM((T_DEV, D), bf16),
            grad,
            grad,
            grad,
        ),
        in_specs=[hbm] * 5,
        out_specs=(vm, vm, vm, vm, vm),
        scratch_shapes=scratch,
        compiler_params=pltpu.CompilerParams(collective_id=0, has_side_effects=True, vmem_limit_bytes=48 * 2**20),
        cost_estimate=pl.CostEstimate(flops=10**10, bytes_accessed=10**7, transcendentals=1024),
        name="step",
    )(*[pltpu.with_memory_space_constraint(a, pltpu.HBM) for a in args])
    return pl.pallas_call(
        write_out,
        out_shape=[jax.ShapeDtypeStruct(o.shape, o.dtype) for o in outs],
        in_specs=[vm] * 5,
        out_specs=[any_] * 5,
        scratch_shapes=[pltpu.SemaphoreType.DMA((5,))],
        compiler_params=pltpu.CompilerParams(vmem_limit_bytes=2**20),
        name="write_out",
    )(*[pltpu.with_memory_space_constraint(o, pltpu.VMEM) for o in outs])


def solution(mesh):
    both = P(("rep", "seq"), None)
    rep = P("rep", None)
    return jax.shard_map(
        body, mesh=mesh, in_specs=(both, rep, rep, rep, both), out_specs=(both,) * 5, check_vma=False
    )
```

```python
import math

import jax
import jax.numpy as jnp
from jax import lax
from jax.experimental import pallas as pl
from jax.experimental.pallas import tpu as pltpu
from jax.sharding import PartitionSpec as P

D = 4096
HD = 128
T_DEV = 512
EPS = 1e-06
MESH = pl.DeviceIdType.MESH
f32 = jnp.float32
bf16 = jnp.bfloat16
N_SEM = 53
BLK = (8, 2, 4, 2, 32, 128)


def mod(a, n):
    return lax.rem(a, jnp.int32(n))


def dot(a, b, ca=1, cb=0):
    return lax.dot_general(a, b, (((ca,), (cb,)), ((), ())), preferred_element_type=f32)


def split(a):
    hi = a.astype(bf16)
    return hi, (a - hi.astype(f32)).astype(bf16)


class Batch:
    def __init__(self, net):
        self.net, self.i, self.copies, self.units = net, net.n, [], 0
        net.n += 1
        assert net.n <= N_SEM
        net.batches.append(self)

    def send(self, src, dst, to):
        cp = self.net.make(src, dst, to, self.i)
        cp.start()
        self.copies.append(cp)
        self.units += math.prod(src.shape) // 2048

    def all(self):
        if len(self.copies) == 1:
            return self.copies[0]
        ref = self.net.sizes.at[pl.ds(0, self.units)]
        return self.net.make(ref, ref, self.net.anyone, self.i)

    def wait(self):
        self.all().wait_recv()


class Net:
    def __init__(self, send_sems, recv_sems, sizes, anyone):
        self.ss, self.rs, self.sizes, self.anyone = send_sems, recv_sems, sizes, anyone
        self.n, self.batches, self.maybe = 0, [], []

    def make(self, src, dst, to, i):
        return pltpu.make_async_remote_copy(
            src_ref=src, dst_ref=dst, send_sem=self.ss.at[i], recv_sem=self.rs.at[i], device_id=to, device_id_type=MESH
        )

    def one(self, src, dst, to):
        b = Batch(self)
        b.send(src, dst, to)
        return b

    def some(self, sends):
        b = Batch(self)
        for src, dst, to in sends:
            b.send(src, dst, to)
        return b

    def send_if(self, cond, src, dst, to, i):
        cp = self.make(src, dst, to, i)
        pl.when(cond)(cp.start)
        self.maybe.append((cp, cond))
        return cp

    def finish(self):
        for b in self.batches:
            b.all().wait_send()
        for cp, cond in self.maybe:
            pl.when(cond)(cp.wait_send)


OFF = (0, 1, 7, 2, 6, 3, 5, 4)
SLOT = {k: p for p, k in enumerate(OFF)}
GROUPS = ((0, 1), (1, 3), (3, 5), (5, 8))


def back(k):
    return (8 - k) % 8


def kernel(
    tok_hbm, wq, wk, wv, cot, att_o, gt_o, gq_o, gk_o, gv_o,
    tok, w0, w1, w2, o0, o1, o2, acc, qkv, cotb, scores, mixl, d_loc, dmix, d_all, d_oth, att_oth, att_snd,
    st_snd, st_rcv, bk_snd, bk_rcv, prior, later,
    p0, p1, p2, sa, ra, acc_a, acc_b, acc_c,
    sa_x, ra_x, sb_y, rb_y, sb_z, rb_z, acc_b2, sc_x, rc_x, sc_z, rc_z, acc_c2,
    sb_d, rb_d, sc_d, rc_d, sizes, send_sems, recv_sems, loc_sems,
):
    rep, seq = lax.axis_index("rep"), lax.axis_index("seq")
    z, yh = lax.div(rep, jnp.int32(2)), mod(rep, 2)
    x, yl, c = lax.div(seq, jnp.int32(4)), mod(lax.div(seq, jnp.int32(2)), 2), mod(seq, 2)
    y = yh * 2 + yl
    oc, oyh = 1 - c, 1 - yh

    def dev(x_, y_, z_, c_):
        return {"rep": z_ * 2 + lax.div(y_, jnp.int32(2)), "seq": x_ * 4 + mod(y_, 2) * 2 + c_}

    def xd(k):
        return dev(mod(x + k, 4), y, z, c)

    def yd(k):
        return dev(x, mod(y + k, 4), z, c)

    def zd(k):
        return dev(x, y, mod(z + k, 8), c)

    partner = dev(x, y, z, oc)
    across = dev(x, 3 - y, z, c)
    group = [(dx, dl) for dx in (2, 1, 3, 0) for dl in (1, 0) if dx or dl]

    def gd(dx, dl):
        return dev(mod(x + dx, 4), yh * 2 + mod(yl + dl, 2), z, c)

    def place(dx, dl):
        return mod(x + dx, 4) * 2 + mod(yl + dl, 2)

    here = x * 2 + yl
    xm, xp = mod(x + 3, 4), mod(x + 1, 4)
    ym, yp = mod(y + 3, 4), mod(y + 1, 4)
    ymh, yml, yph, ypl = lax.div(ym, jnp.int32(2)), mod(ym, 2), lax.div(yp, jnp.int32(2)), mod(yp, 2)
    lane_c = pl.ds(pl.multiple_of(c * HD, HD), HD)
    lane_o = pl.ds(pl.multiple_of(oc * HD, HD), HD)
    mine = pl.ds(pl.multiple_of(c * 512, 512), 512)

    def cols(p):
        return pl.ds(pl.multiple_of(mod(z + OFF[p], 8) * 512, 512), 512)

    plane = [(dx, dy) for dx in (2, 1, 3, 0) for dy in (2, 1, 3, 0) if dx or dy]
    peers = [partner] + [dev(x, y, mod(z + k, 8), c_) for k in (4, 3, 5, 2, 6, 1, 7) for c_ in (c, oc)]
    peers += [dev(mod(x + dx, 4), mod(y + dy, 4), z, c_) for dx, dy in plane for c_ in (c, oc)]
    bar = pltpu.get_barrier_semaphore()
    for to in peers:
        pl.semaphore_signal(bar, inc=1, device_id=to, device_id_type=MESH)
    loads = [
        pltpu.make_async_copy(src, dst, loc_sems.at[i])
        for i, (src, dst) in enumerate(
            (
                (wk.at[x, yl, :, lane_c], w1.at[0, yh, x, yl]),
                (wv.at[x, yl, :, lane_c], w2.at[0, yh, x, yl]),
                (wq.at[:, :, :, lane_c], w0.at[0, yh]),
                (tok_hbm, tok.at[mine]),
                (cot.at[:, lane_c], cotb.at[c]),
            )
        )
    ]
    for cp in loads:
        cp.start()
    for cp in loads[:3]:
        cp.wait()
    pl.semaphore_wait(bar, len(peers))

    net = Net(send_sems, recv_sems, sizes, partner)

    ga, gb, gc, ge = GROUPS
    steps = {g: Batch(net) for g in GROUPS[1:]}
    for k in (1, 7, 2, 6, 3, 5, 4):
        to = SLOT[back(k)]
        for g in GROUPS[1:]:
            if to in range(*g):
                for w in (w1, w2):
                    steps[g].send(w.at[0, yh, x, yl], w.at[to, yh, x, yl], zd(k))

    def slots(g):
        return pl.ds(g[0], g[1] - g[0])

    def mid(g):
        if g in steps:
            steps[g].wait()
        b, c_ = w1.at[slots(g), yh, x, yl], w2.at[slots(g), yh, x, yl]
        return net.some([t for k in (1, 3, 2) for t in ((b, b, yd(k)), (c_, c_, xd(k)))])

    def wide(g, prev):
        prev.wait()
        b = [w1.at[slots(g), h, x] for h in (0, 1)]
        c_ = [w2.at[slots(g), yh, pl.ds(2 * h, 2), yl] for h in (0, 1)]
        lead = net.some([t for h, k in ((0, 1), (1, 3)) for t in ((b[h], b[h], xd(k)), (c_[h], c_[h], yd(k)))])
        rest = net.some([t for h, k in ((1, 1), (0, 3)) for t in ((b[h], b[h], xd(k)), (c_[h], c_[h], yd(k)))])
        return lead, rest

    def pass_on(g, prev):
        lead, rest = prev
        lead.wait()
        for ref, to in (
            (w1.at[slots(g), 0, xm], xd(1)),
            (w1.at[slots(g), 1, xp], xd(3)),
            (w2.at[slots(g), ymh, pl.ds(0, 2), yml], yd(1)),
            (w2.at[slots(g), yph, pl.ds(2, 2), ypl], yd(3)),
        ):
            rest.send(ref, ref, to)
        return rest

    def a_send(k, *parts):
        sends = []
        for half, way in parts:
            at, to = (back(k), back(k + 1)) if way == 0 else (k, k + 1)
            sends.append((w0.at[SLOT[at], half], w0.at[SLOT[to], half], zd(1 if way == 0 else 7)))
        return net.some(sends)

    def a_half(prev, half, k):
        prev.wait()
        return a_send(k, (half, 0), (half, 1))

    m_a = mid(ga)
    a_y = net.one(w0.at[0, yh], w0.at[0, yh], across)
    a1 = [a_send(0, (yh, 0), (yh, 1))]
    cot_x = net.one(cot.at[:, lane_o], cotb.at[c], partner)
    tok_x = net.one(tok_hbm, tok.at[mine], partner)

    rows = [slice(0, 512), slice(512, 1024)]

    def project(ps, lanes, ws, first):
        for r in rows:
            got = None
            for p in ps:
                w = jnp.concatenate([w[p].reshape(512, HD) for w in ws], 1)
                term = dot(tok[r, cols(p)], w)
                got = term if got is None else got + term
            acc[r, lanes] = got if first else acc[r, lanes] + got

    def q_acc(*ps):
        project(ps, slice(0, 128), (w0,), ps[0] == 0)

    def kv_acc(g):
        project(range(*g), slice(128, 384), (w1, w2), g[0] == 0)

    m_b = mid(gb)
    n_a = wide(ga, m_a)
    a_y.wait()
    a1.append(a_send(0, (oyh, 0), (oyh, 1)))
    m_c = mid(gc)
    m_e = mid(ge)
    n_b = wide(gb, m_b)
    a2 = [a_half(a1[0], yh, 1)]
    f_a = pass_on(ga, n_a)
    n_c = wide(gc, m_c)
    a2.append(a_half(a1[1], oyh, 1))
    n_e = wide(ge, m_e)
    f_b = pass_on(gb, n_b)
    loads[3].wait()
    tok_x.wait()
    f_a.wait()
    kv_acc(ga)
    f_c = pass_on(gc, n_c)
    a3 = [a_half(a2[0], yh, 2)]
    q_acc(0)
    q_acc(1, 2)
    f_e = pass_on(ge, n_e)
    a3.append(a_half(a2[1], oyh, 2))
    f_b.wait()
    kv_acc(gb)
    f_c.wait()
    kv_acc(gc)
    for cp in a3:
        cp.wait()
    a4 = a_send(3, (0, 0), (1, 1))
    f_e.wait()
    w_x = [net.one(w1, o1, partner), net.one(w2, o2, partner)]
    kv_acc(ge)

    state = []
    for r in rows:
        qkv[r, 128:384] = acc[r, 128:384].astype(bf16)
        state.append(dot(qkv[r, 128:256], qkv[r, 256:384], 0, 0))
    st_snd[...] = (state[0] + state[1]).astype(bf16)
    prior[0] = jnp.zeros((HD, HD), f32)
    prior[1] = state[0]
    pair = net.n
    net.n += len(group)
    st = [
        net.send_if(place(dx, dl) > here, st_snd, st_rcv.at[i], gd(dx, dl), pair + i) for i, (dx, dl) in enumerate(group)
    ]

    q_acc(3, 4, 5, 6)
    a4.wait()
    w_x.append(net.one(w0, o0, partner))
    q_acc(7)
    qkv[:, 0:128] = acc[:, 0:128].astype(bf16)
    causal = lax.broadcasted_iota(jnp.int32, (512, 512), 0) >= lax.broadcasted_iota(jnp.int32, (512, 512), 1)
    for b, r in enumerate(rows):
        scores[b] = jnp.where(causal, dot(qkv[r, 0:128], qkv[r, 128:256], 1, 1), 0.0).astype(bf16)
        mixl[b] = dot(scores[b], qkv[r, 256:384])
    loads[4].wait()
    cot_x.wait()
    for i, (dx, dl) in enumerate(group):

        @pl.when(place(4 - dx, dl) < here)
        def _(i=i):
            st[i].wait_recv()
            got = st_rcv[i].astype(f32)
            prior[0] += got
            prior[1] += got

    back_state = []
    for b, r in enumerate(rows):
        p_hi, p_lo = split(prior[b])
        q = qkv[r, 0:128]
        mix = mixl[b] + (dot(q, p_hi) + dot(q, p_lo))
        s = lax.rsqrt(jnp.mean(mix * mix, -1, keepdims=True) + EPS)
        att_snd[b] = (mix * s).astype(bf16)
        g = cotb[b].astype(f32)
        m = jnp.mean(g * mix, -1, keepdims=True)
        dmix[b] = (s * g - s * s * s * mix * m).astype(bf16)
        back_state.append(dot(q, dmix[b], 0, 0))
    bk_snd[...] = (back_state[0] + back_state[1]).astype(bf16)
    later[1] = jnp.zeros((HD, HD), f32)
    later[0] = back_state[1]
    bk = [
        net.send_if(place(dx, dl) < here, bk_snd, bk_rcv.at[i], gd(dx, dl), pair + i) for i, (dx, dl) in enumerate(group)
    ]
    att_x = net.one(att_snd.at[oc], att_oth, partner)

    for b, r in enumerate(rows):
        q, k, v = qkv[r, 0:128], qkv[r, 128:256], qkv[r, 256:384]
        bs = jnp.where(causal, dot(dmix[b], v, 1, 1), 0.0).astype(bf16)
        p_hi, p_lo = split(prior[b])
        d_all[r, 0:128] = (dot(bs, k) + (dot(dmix[b], p_hi, 1, 1) + dot(dmix[b], p_lo, 1, 1))).astype(bf16)
        mixl[b] = dot(bs, q, 0, 0)
        d_loc[b] = dot(scores[b], dmix[b], 0, 0)

    def p_q(p):
        p0[p] = dot(tok[:, cols(p)], d_all[:, 0:128], 0, 0).reshape(BLK[1:])

    def p_kv(g):
        for p in range(*g):
            got = dot(tok[:, cols(p)], d_all[:, 128:384], 0, 0)
            p1[p] = got[:, 0:128].reshape(BLK[1:])
            p2[p] = got[:, 128:256].reshape(BLK[1:])

    def p_qkv(g):
        for p in range(*g):
            got = dot(tok[:, cols(p)], d_all[...], 0, 0)
            p0[p] = got[:, 0:128].reshape(BLK[1:])
            p1[p] = got[:, 128:256].reshape(BLK[1:])
            p2[p] = got[:, 256:384].reshape(BLK[1:])

    def a_out(step, parts, plus=None):
        if plus is not None:
            plus.wait()
        sends = []
        for way, half in parts:
            k = 5 - step
            val = p0[SLOT[k if way == 0 else 8 - k], half]
            if plus is not None:
                val = val + ra[way, step - 2, half].astype(f32)
            sa[way, step - 1, half] = val.astype(bf16)
            sends.append((sa.at[way, step - 1, half], ra.at[way, step - 1, half], zd(1 if way == 0 else 7)))
        return net.some(sends)

    ends, free = ((0, 0), (1, 1)), ((0, 1), (1, 0))
    p_q(7)
    r1 = a_out(1, ends)
    p_q(5)
    p_q(6)
    r2f = a_out(2, free)
    p_q(3)
    p_q(4)

    for i, (dx, dl) in enumerate(group):

        @pl.when(place(4 - dx, dl) > here)
        def _(i=i):
            bk[i].wait_recv()
            got = bk_rcv[i].astype(f32)
            later[0] += got
            later[1] += got

    r2 = a_out(2, ends, r1)
    for b, r in enumerate(rows):
        l_hi, l_lo = split(later[b])
        k, v = qkv[r, 128:256], qkv[r, 256:384]
        d_all[r, 128:256] = (mixl[b] + (dot(v, l_hi, 1, 1) + dot(v, l_lo, 1, 1))).astype(bf16)
        d_all[r, 256:384] = (d_loc[b] + (dot(k, l_hi) + dot(k, l_lo))).astype(bf16)
    d_x = net.one(d_all.at[pl.ds(pl.multiple_of(oc * 512, 512), 512)], d_oth, partner)

    def direct(g):
        out = Batch(net)
        for k in (2, 1, 3):
            sb_d[k - 1, slots(g)] = p1[slots(g), :, mod(x + k, 4)].astype(bf16)
            out.send(sb_d.at[k - 1, slots(g)], rb_d.at[k - 1, slots(g)], xd(k))
            at = mod(y + k, 4)
            sc_d[k - 1, slots(g)] = p2[slots(g), lax.div(at, jnp.int32(2)), :, mod(at, 2)].astype(bf16)
            out.send(sc_d.at[k - 1, slots(g)], rc_d.at[k - 1, slots(g)], yd(k))
        return out

    def third(g, prev):
        prev.wait()
        acc_b[slots(g)] = p1[slots(g), :, x] + sum(rb_d[k, slots(g)].astype(f32) for k in range(3))
        acc_c[slots(g)] = p2[slots(g), yh, :, yl] + sum(rc_d[k, slots(g)].astype(f32) for k in range(3))
        out = Batch(net)
        for k in (2, 1, 3):
            at = mod(y + k, 4)
            sb_y[k - 1, slots(g)] = acc_b[slots(g), lax.div(at, jnp.int32(2)), mod(at, 2)].astype(bf16)
            out.send(sb_y.at[k - 1, slots(g)], rb_y.at[k - 1, slots(g)], yd(k))
            sc_x[k - 1, slots(g)] = acc_c[slots(g), mod(x + k, 4)].astype(bf16)
            out.send(sc_x.at[k - 1, slots(g)], rc_x.at[k - 1, slots(g)], xd(k))
        return out

    last = Batch(net)

    def fourth(g, prev):
        prev.wait()
        n = g[1] - g[0]
        got = acc_b[slots(g), yh, yl] + sum(rb_y[k, slots(g)].astype(f32) for k in range(3))
        acc_b2[slots(g)] = got.reshape(n, 2, 16, HD)
        got = acc_c[slots(g), x] + sum(rc_x[k, slots(g)].astype(f32) for k in range(3))
        acc_c2[slots(g)] = got.reshape(n, 2, 16, HD)
        for snd, rcv, total in ((sb_z, rb_z, acc_b2), (sc_z, rc_z, acc_c2)):
            snd[slots(g)] = total[slots(g)].astype(bf16)
            for p in range(*g):
                k = OFF[p]
                to = SLOT[back(k)]
                if k:
                    last.send(snd.at[p, c], rcv.at[0, to], zd(k))
                last.send(snd.at[p, oc], rcv.at[1, to], dev(x, y, mod(z + k, 8), oc) if k else partner)

    def g_t(*ps):
        for p in ps:
            w = jnp.concatenate([ref[p].reshape(512, HD) for ref in (w0, w1, w2, o0, o1, o2)], 1)
            d = jnp.concatenate([d_all[mine, :], d_oth[...]], 1)
            gt_o[:, cols(p)] = dot(d, w, 1, 1).astype(bf16)

    p_kv(ge)
    d_e = direct(ge)
    p_kv(gc)
    d_c = direct(gc)
    r3f = a_out(3, free, r2f)
    p_qkv(gb)
    d_b = direct(gb)
    r3 = a_out(3, ends, r2)
    p_qkv(ga)
    d_a = direct(ga)
    d_x.wait()
    for cp in w_x:
        cp.wait()
    g_t(0)
    r4f = a_out(4, free, r3f)
    r4 = a_out(4, ends, r3)
    g_t(1)
    t_e = third(ge, d_e)
    g_t(2)
    t_c = third(gc, d_c)
    g_t(3)
    t_b = third(gb, d_b)
    t_a = third(ga, d_a)
    r4f.wait()
    r4.wait()
    acc_a[...] = (p0[0] + ra[0, 3].astype(f32) + ra[1, 3].astype(f32)).reshape(2, 4, 2, 2, 16, HD)
    sa_x[...] = acc_a[...].astype(bf16)
    for i, (dx, dy) in enumerate(plane):
        ax, ay = mod(x + dx, 4), mod(y + dy, 4)
        part = sa_x.at[lax.div(ay, jnp.int32(2)), ax, mod(ay, 2)]
        last.send(part.at[c], ra_x.at[0, i], dev(ax, ay, z, c))
        last.send(part.at[oc], ra_x.at[1, i], dev(ax, ay, z, oc))
    last.send(sa_x.at[yh, x, yl, oc], ra_x.at[1, 15], partner)
    fourth(ge, t_e)
    fourth(gc, t_c)
    g_t(4)
    fourth(gb, t_b)
    g_t(5)
    fourth(ga, t_a)
    g_t(6, 7)
    att_o[:, lane_c] = att_snd[c]
    att_x.wait()
    att_o[:, lane_o] = att_oth[...]
    scale = 1.0 / T_DEV
    last.wait()
    gq_o[:, lane_c] = (acc_a[yh, x, yl, c] + sum(ra_x[0, k].astype(f32) for k in range(15))) * scale
    gq_o[:, lane_o] = sum(ra_x[1, k].astype(f32) for k in range(16)) * scale
    for out, total, rcv in ((gk_o, acc_b2, rb_z), (gv_o, acc_c2, rc_z)):
        out[:, lane_c] = (total[0, c] + sum(rcv[0, p].astype(f32) for p in range(1, 8))) * scale
        out[:, lane_o] = sum(rcv[1, p].astype(f32) for p in range(8)) * scale
    net.finish()


def write_out(*refs):
    sems = refs[10]
    copies = [pltpu.make_async_copy(refs[i], refs[5 + i], sems.at[i]) for i in (1, 0, 2, 3, 4)]
    for cp in copies:
        cp.start()
    for cp in copies:
        cp.wait()


def body(tokens, w_query, w_key, w_value, cotangent):
    vm, any_ = pl.BlockSpec(memory_space=pltpu.VMEM), pl.BlockSpec(memory_space=pl.ANY)
    hbm = pl.BlockSpec(memory_space=pltpu.HBM)

    def v(*shape, t=bf16):
        return pltpu.VMEM(shape, t)

    scratch = [v(1024, D)] + [v(*BLK)] * 6
    scratch += [v(1024, 384, t=f32), v(1024, 384), v(2, 512, 128), v(2, 512, 512), v(2, 512, 128, t=f32), v(2, 512, 128, t=f32), v(2, 512, 128)]
    scratch += [v(1024, 384), v(512, 384), v(512, 128), v(2, 512, 128)]
    scratch += [v(128, 128), v(7, 128, 128), v(128, 128), v(7, 128, 128), v(2, 128, 128, t=f32), v(2, 128, 128, t=f32)]
    scratch += [v(*BLK, t=f32)] * 3
    scratch += [v(2, 4, 2, 4, 2, 32, 128)] * 2
    scratch += [v(2, 4, 2, 2, 16, 128, t=f32), v(8, 2, 2, 32, 128, t=f32), v(8, 4, 32, 128, t=f32)]
    scratch += [v(2, 4, 2, 2, 16, 128), v(2, 16, 16, 128)]
    scratch += [v(3, 8, 32, 128)] * 2 + [v(8, 2, 16, 128), v(2, 8, 16, 128)] + [v(8, 2, 16, 128, t=f32)]
    scratch += [v(3, 8, 32, 128)] * 2 + [v(8, 2, 16, 128), v(2, 8, 16, 128)] + [v(8, 2, 16, 128, t=f32)]
    scratch += [v(3, 8, 2, 2, 32, 128)] * 2 + [v(3, 8, 4, 32, 128)] * 2 + [v(160, 16, 128)]
    scratch += [pltpu.SemaphoreType.DMA((N_SEM,)), pltpu.SemaphoreType.DMA((N_SEM,)), pltpu.SemaphoreType.DMA((5,))]
    grad = pltpu.VMEM((16, 256), f32)
    args = [tokens] + [w.reshape(4, 2, 32, 256) for w in (w_query, w_key, w_value)] + [cotangent]
    outs = pl.pallas_call(
        kernel,
        out_shape=(
            pltpu.VMEM((T_DEV, 256), bf16),
            pltpu.VMEM((T_DEV, D), bf16),
            grad,
            grad,
            grad,
        ),
        in_specs=[hbm] * 5,
        out_specs=(vm, vm, vm, vm, vm),
        scratch_shapes=scratch,
        compiler_params=pltpu.CompilerParams(collective_id=0, has_side_effects=True, vmem_limit_bytes=48 * 2**20),
        cost_estimate=pl.CostEstimate(flops=10**10, bytes_accessed=10**7, transcendentals=1024),
        name="step",
    )(*[pltpu.with_memory_space_constraint(a, pltpu.HBM) for a in args])
    return pl.pallas_call(
        write_out,
        out_shape=[jax.ShapeDtypeStruct(o.shape, o.dtype) for o in outs],
        in_specs=[vm] * 5,
        out_specs=[any_] * 5,
        scratch_shapes=[pltpu.SemaphoreType.DMA((5,))],
        compiler_params=pltpu.CompilerParams(vmem_limit_bytes=2**20),
        name="write_out",
    )(*[pltpu.with_memory_space_constraint(o, pltpu.VMEM) for o in outs])


def solution(mesh):
    both = P(("rep", "seq"), None)
    rep = P("rep", None)
    return jax.shard_map(
        body, mesh=mesh, in_specs=(both, rep, rep, rep, both), out_specs=(both,) * 5, check_vma=False
    )
```
